256 devices in a mesh: row: 32 (over z, y_hi, core), col: 8 (over x, y_lo).
Axes of the slice: x: 4, y: 4 (y_hi: 2, y_lo: 2; y = y_hi * 2 + y_lo), z: 8, core: 2. Of those that a mesh axis runs over, the one named last changes fastest.
Arguments:
- left_blocks: bfloat16 [128, 64, 128, 128], P('row', 'col'), may hold values from -0.25 to 0.25
- left_index: int32 [128, 64], P('row', 'col'), may hold values from 0 to 3, as said below
- left_count: int32 [128, 32], P('row', 'col'), may hold values from 0 to 2
- right_blocks: bfloat16 [128, 24, 128, 128], P('row', 'col'), may hold values from -6 to 6
- right_index: int32 [128, 24], P('row', 'col'), may hold values from 0 to 15, as said below
- right_count: int32 [128, 8], P('row', 'col'), may hold values from 0 to 3
- product_index: int32 [128, 48], P('row', 'col'), may hold values from 0 to 15, as said below
- product_count: int32 [128, 8], P('row', 'col'), may hold values from 1 to 6
Outputs:
- product_blocks: float32 [128, 48, 128, 128], P('row', 'col')
The draws below stay inside these ranges and needn't reach their ends.
Inputs may be any that keep to these rules, and one draw needn't show every extreme that they name: `left_index`: within one block row and one range, the 2 indices of the slots are distinct, dead slots included. `right_index`: within one block row and one index of col, the 3 indices are distinct, dead slots included. `product_index`: within one block row and one index of col, the 6 indices are distinct, unused slots included.
All inputs are finite; a program needn't handle non-finite values.
Results may differ from the reference program's by a relative error of at most 0.0003.
Values may be sent and summed in bfloat16 or wider, within the bound.
A program may use at most 256 MiB of HBM per device.

```python
import jax
import jax.numpy as jnp
from jax import lax

BLOCK = 128
ROWS_DEV = 4
LEFT_SLOTS = 2
RIGHT_SLOTS = 3
OUT_SLOTS = 6
NBLK = 128
N_ROW = 32
N_COL = 8


def distinct_slots(key, groups, pick, span):
    scores = jax.random.randint(key, (NBLK, groups, span), 0, 1 << 20) * span + jnp.arange(span, dtype=jnp.int32)
    order = jnp.argsort(scores, axis=-1, stable=True)[:, :, :pick]
    return order.reshape(NBLK, groups * pick).astype(jnp.int32)


def capped_counts(key, groups, lowest, most):
    counts = jax.random.randint(key, (NBLK, groups), lowest, most + 1)
    return counts.at[0, 0].set(most).astype(jnp.int32)


def draw_left_index(key, part):
    key = jax.random.fold_in(key, 11)
    return distinct_slots(key, N_ROW, LEFT_SLOTS, ROWS_DEV)


def draw_left_count(key, part):
    key = jax.random.fold_in(key, 12)
    return capped_counts(key, N_ROW, 0, LEFT_SLOTS)


def draw_right_index(key, part):
    key = jax.random.fold_in(key, 13)
    return distinct_slots(key, N_COL, RIGHT_SLOTS, NBLK // N_COL)


def draw_right_count(key, part):
    key = jax.random.fold_in(key, 14)
    return capped_counts(key, N_COL, 0, RIGHT_SLOTS)


def draw_product_index(key, part):
    key = jax.random.fold_in(key, 15)
    return distinct_slots(key, N_COL, OUT_SLOTS, NBLK // N_COL)


def draw_product_count(key, part):
    key = jax.random.fold_in(key, 16)
    return capped_counts(key, N_COL, 1, OUT_SLOTS)


def shard_levels(rng, extent, pieces, smallest, top_value):
    loudness = 1.0
    for axis_at, shards_of in pieces:
        heights = jax.random.uniform(jax.random.fold_in(jax.random.fold_in(rng, 6), axis_at), (shards_of,), jnp.float32, smallest / len(pieces), top_value / len(pieces))
        loudness = loudness * jnp.repeat(jnp.exp(heights), extent[axis_at] // shards_of).reshape((-1,) + (1,) * (len(extent) - 1 - axis_at))
    return loudness


def normal_values(rng, extent, deviation, most, shards=(), held_as=jnp.bfloat16):
    level = shard_levels(rng, extent, shards, -0.22, 0.18) if shards else 1.0
    values = jax.random.normal(rng, extent, jnp.float32) * deviation * level
    return jnp.minimum(jnp.maximum(values, -most), most).astype(held_as)


def setup_inputs(seed: int = 0) -> dict:
    arg_keys = jax.random.split(jax.random.key(seed), 9)
    left_blocks = normal_values(arg_keys[0], (NBLK, N_ROW * LEFT_SLOTS, BLOCK, BLOCK), (4 * BLOCK) ** -0.5, 0.25, ((0, 32), (1, 8)))
    left_index = draw_left_index(jax.random.fold_in(arg_keys[8], 71), 0)
    left_count = draw_left_count(jax.random.fold_in(arg_keys[8], 71), 0)
    right_blocks = normal_values(arg_keys[3], (NBLK, N_COL * RIGHT_SLOTS, BLOCK, BLOCK), 1.0, 6.0, ((0, 32), (1, 8)))
    right_index = draw_right_index(jax.random.fold_in(arg_keys[8], 71), 0)
    right_count = draw_right_count(jax.random.fold_in(arg_keys[8], 71), 0)
    product_index = draw_product_index(jax.random.fold_in(arg_keys[8], 71), 0)
    product_count = draw_product_count(jax.random.fold_in(arg_keys[8], 71), 0)
    return dict(left_blocks=left_blocks, left_index=left_index, left_count=left_count, right_blocks=right_blocks, right_index=right_index, right_count=right_count, product_index=product_index, product_count=product_count)


def reference(left_blocks, left_index, left_count, right_blocks, right_index, right_count, product_index, product_count):
    left_slot = jnp.arange(N_ROW * LEFT_SLOTS, dtype=jnp.int32)
    left_live = ((left_slot % LEFT_SLOTS)[None, :] < jnp.repeat(left_count, LEFT_SLOTS, axis=1)).astype(jnp.int32)
    left_column = (left_slot // LEFT_SLOTS)[None, :] * ROWS_DEV + left_index
    right_slot = jnp.arange(N_COL * RIGHT_SLOTS, dtype=jnp.int32)
    right_live = ((right_slot % RIGHT_SLOTS)[None, :] < jnp.repeat(right_count, RIGHT_SLOTS, axis=1)).astype(jnp.int32)
    out_slot = jnp.arange(N_COL * OUT_SLOTS, dtype=jnp.int32)
    out_live = ((out_slot % OUT_SLOTS)[None, :] < jnp.repeat(product_count, OUT_SLOTS, axis=1)).astype(jnp.int32)

    def one_row(items):
        blocks, columns, live, wanted, kept = items
        chosen = right_blocks[columns]
        partial_value = jnp.einsum("sab,stbc->stac", blocks.astype(jnp.float32), chosen.astype(jnp.float32),
                             precision=lax.Precision.HIGHEST)
        valid = (live[:, None] > 0) & (right_live[columns] > 0)
        found = right_index[columns].reshape(-1, N_COL, RIGHT_SLOTS)
        target = wanted.reshape(N_COL, OUT_SLOTS)
        match = (found[:, :, :, None] == target[None, :, None, :]) & valid.reshape(-1, N_COL, RIGHT_SLOTS)[:, :, :, None]
        match = match & (kept.reshape(N_COL, OUT_SLOTS) > 0)[None, :, None, :]
        partial_value = partial_value.reshape(-1, N_COL, RIGHT_SLOTS, BLOCK, BLOCK)
        summed = jnp.einsum("sctu,sctab->cuab", match.astype(jnp.float32), partial_value,
                            precision=lax.Precision.HIGHEST)
        return summed.reshape(N_COL * OUT_SLOTS, BLOCK, BLOCK)

    return lax.map(one_row, (left_blocks, left_column, left_live, product_index, out_live))
```

```python
import functools

import jax
import jax.numpy as jnp
from jax import lax
from jax.experimental import pallas as pl
from jax.experimental.pallas import tpu as pltpu
from jax.sharding import PartitionSpec as P

MESH = pl.DeviceIdType.MESH
BLK = 128
NZ, NX = 8, 4
ROWS, LSLOT, RSLOT, OSLOT = 4, 8, 3, 6
RDEV = ROWS * RSLOT
GROUP = 4 * RDEV
ZERO = GROUP


def kernel(lidx, lcnt, ridx, rcnt, pidx, pcnt, left, right, out, lbuf, *rest):
    rg = rest[:NZ]
    rm, rs, rc, lm, ls, lc, code_v, code, lk, send, recv, local = rest[NZ:]
    row, col = lax.axis_index("row"), lax.axis_index("col")
    z, h, e = row // 4, (row // 2) % 2, row % 2
    x, y = col // 2, col % 2
    g = h * 2 + e

    def zdev(d):
        return (((z + d) % NZ) * 4 + g, col)

    def xdev(d):
        return (row, ((x + d) % NX) * 2 + y)

    hdev = (z * 4 + (1 - h) * 2 + e, col)
    edev = (z * 4 + h * 2 + (1 - e), col)
    ydev = (row, x * 2 + (1 - y))

    barrier = pltpu.get_barrier_semaphore()
    partners = [zdev(d) for d in range(1, NZ)] + [xdev(d) for d in range(1, NX)] + [hdev, edev, ydev]
    for dev in partners:
        pl.semaphore_signal(barrier, inc=1, device_id=dev, device_id_type=MESH)

    own_left = pltpu.make_async_copy(left, lbuf.at[col], local.at[0])
    own_left.start()
    own_right = pltpu.make_async_copy(right, rg[0].at[pl.ds(g * RDEV, RDEV)], local.at[1])
    own_right.start()

    sub = lax.broadcasted_iota(jnp.int32, (8, BLK), 0)
    lane = lax.broadcasted_iota(jnp.int32, (8, BLK), 1)
    table = jnp.zeros((8, BLK), jnp.int32)
    for j in range(ROWS):
        for t in range(RSLOT):
            value = jnp.where(t < rcnt[j, 0], ridx[j, t] + 1, 0)
            table = jnp.where((sub == t) & (lane == row * ROWS + j), value, table)
    rm[0] = table
    table = jnp.zeros((8, BLK), jnp.int32)
    for i in range(ROWS):
        for s in range(LSLOT):
            value = jnp.where(s % 2 < lcnt[i, s // 2], (col * 4 + s // 2) * ROWS + lidx[i, s] + 1, 0)
            table = jnp.where((sub == i) & (lane == col * LSLOT + s), value, table)
    lm[0] = table

    pl.semaphore_wait(barrier, len(partners))

    copies = {}

    def push(name, src, dst, dev):
        n = len(copies)
        copy = pltpu.make_async_remote_copy(
            src_ref=src,
            dst_ref=dst,
            send_sem=send.at[n],
            recv_sem=recv.at[n],
            device_id=dev,
            device_id_type=MESH,
        )
        copy.start()
        copies[name] = copy

    def arrived(*names):
        for name in names:
            copies[name].wait_recv()

    def rpart(d, hh, first=0, size=RDEV):
        return rg[d % NZ].at[pl.ds((hh * 2 + e) * RDEV + first, size)]

    def lpart(dx, yy, half=None):
        at = ((x + dx) % NX) * 2 + yy
        if half is None:
            return lbuf.at[at]
        return lbuf.at[at, pl.ds(2 * half, 2)]

    push("ma", rm.at[0], rm.at[1], edev)
    push("na", lm.at[0], lm.at[1], ydev)
    push("r+1o", right, rpart(-1, h), zdev(1))
    push("r-1o", right, rpart(1, h), zdev(-1))
    push("rh", right, rpart(0, h), hdev)
    push("l+1", left, lpart(0, y), xdev(1))
    push("l-1", left, lpart(0, y), xdev(-1))
    push("ly", left, lpart(0, y), ydev)
    push("e0o", right, rpart(0, h), edev)

    arrived("ma", "na")
    rs[...] = rm[0] + rm[1]
    ls[...] = lm[0] + lm[1]
    push("mb", rs, rm.at[2], hdev)
    for d in range(1, NX):
        push(f"nb{d}", ls, lc.at[d - 1], xdev(d))
    arrived("mb")
    rs2 = rm.at[3]
    rs2[...] = rs[...] + rm[2]
    for d in range(1, NZ):
        push(f"mc{d}", rs2, rc.at[d - 1], zdev(d))
    for ref in rg:
        ref[ZERO] = jnp.zeros((BLK, BLK), jnp.bfloat16)

    def hop(d, hh, tag):
        arrived(f"r+{d}{tag}", f"r-{d}{tag}")
        if d < 3:
            push(f"r+{d + 1}{tag}", rpart(-d, hh), rpart(-d - 1, hh), zdev(1))
            push(f"r-{d + 1}{tag}", rpart(d, hh), rpart(d + 1, hh), zdev(-1))
        else:
            push(f"r+4{tag}", rpart(-d, hh, 0, 6), rpart(4, hh, 0, 6), zdev(1))
            push(f"r-4{tag}", rpart(d, hh, 6, 6), rpart(4, hh, 6, 6), zdev(-1))
        push(f"e-{d}{tag}", rpart(-d, hh), rpart(-d, hh), edev)
        push(f"e+{d}{tag}", rpart(d, hh), rpart(d, hh), edev)

    def last(hh, tag):
        arrived(f"r+4{tag}", f"r-4{tag}")
        push(f"e4{tag}", rpart(4, hh), rpart(4, hh), edev)

    hop(1, h, "o")
    arrived("rh")
    push("r+1p", rpart(0, 1 - h), rpart(-1, 1 - h), zdev(1))
    push("r-1p", rpart(0, 1 - h), rpart(1, 1 - h), zdev(-1))
    push("e0p", rpart(0, 1 - h), rpart(0, 1 - h), edev)

    arrived(*[f"mc{d}" for d in range(1, NZ)], *[f"nb{d}" for d in range(1, NX)])
    right_table = rs2[...]
    for d in range(NZ - 1):
        right_table = right_table + rc[d]
    left_table = ls[...]
    for d in range(NX - 1):
        left_table = left_table + lc[d]
    lc[NX - 1] = jnp.where(left_table == 0, BLK, left_table - 1)
    wide_sub = lax.broadcasted_iota(jnp.int32, (ROWS * OSLOT, BLK), 0)
    wide_lane = lax.broadcasted_iota(jnp.int32, (ROWS * OSLOT, BLK), 1)
    wanted = jnp.full((ROWS * OSLOT, BLK), -1, jnp.int32)
    for i in range(ROWS):
        for u in range(OSLOT):
            value = jnp.where(u < pcnt[i, 0], pidx[i, u] + 1, -1)
            wanted = jnp.where(wide_sub == i * OSLOT + u, value, wanted)
    found = jnp.full((ROWS * OSLOT, BLK), ZERO, jnp.int32)
    for t in range(RSLOT):
        found = jnp.where(right_table[t : t + 1, :] == wanted, (wide_lane % 16) * RSLOT + t, found)
    code_v[:, :BLK] = found
    code_v[:, BLK:] = jnp.full((ROWS * OSLOT, BLK), ZERO, jnp.int32)
    to_code = pltpu.make_async_copy(code_v, code, local.at[2])
    to_code.start()
    to_lk = pltpu.make_async_copy(lc.at[NX - 1], lk, local.at[3])
    to_lk.start()

    hop(2, h, "o")
    arrived("ly", "l+1", "l-1")
    push("a+1", lpart(0, 1 - y, 0), lpart(0, 1 - y, 0), xdev(1))
    push("a-1", lpart(0, 1 - y, 0), lpart(0, 1 - y, 0), xdev(-1))
    push("b+1", lpart(-1, y, 1), lpart(-1, y, 1), ydev)
    push("b-1", lpart(1, y, 1), lpart(1, y, 1), ydev)
    push("l+2", lpart(-1, y, 0), lpart(-1, y, 0), xdev(1))
    push("l-2", lpart(1, y, 1), lpart(1, y, 1), xdev(-1))
    hop(1, 1 - h, "p")
    hop(3, h, "o")
    arrived("a+1", "a-1", "b+1", "b-1")
    push("a+2", lpart(-1, 1 - y, 0), lpart(-1, 1 - y, 0), xdev(1))
    push("b-2", lpart(1, 1 - y, 1), lpart(1, 1 - y, 1), xdev(-1))
    hop(2, 1 - h, "p")
    last(h, "o")
    hop(3, 1 - h, "p")
    last(1 - h, "p")
    arrived("l+2", "l-2", "a+2", "b-2")
    for tag in "op":
        arrived(f"e0{tag}")
        for d in range(1, 4):
            arrived(f"e-{d}{tag}", f"e+{d}{tag}")
        arrived(f"e4{tag}")
    own_left.wait()
    own_right.wait()
    to_code.wait()
    to_lk.wait()

    out[...] = jnp.zeros_like(out)
    for d in (0, 1, 7, 2, 6, 3, 5, 4):
        c = (z + d) % NZ

        def one_row(i, carry, ref=rg[d], c=c):
            ks = [lk[i, c * LSLOT + s] for s in range(LSLOT)]
            lhs = jnp.concatenate([lbuf[c, i, s] for s in range(LSLOT)], axis=1)
            for u in range(0, OSLOT, 2):
                rhs = jnp.concatenate(
                    [
                        jnp.concatenate([ref[code[i * OSLOT + u + n, ks[s]]] for n in range(2)], axis=1)
                        for s in range(LSLOT)
                    ],
                    axis=0,
                )
                part = jnp.dot(lhs, rhs, preferred_element_type=jnp.float32)
                out[i, u] += part[:, :BLK]
                out[i, u + 1] += part[:, BLK:]
            return carry

        lax.fori_loop(0, ROWS, one_row, 0)

    for copy in copies.values():
        copy.wait_send()


COPIES = 80


def per_device(
    left_blocks,
    left_index,
    left_count,
    right_blocks,
    right_index,
    right_count,
    product_index,
    product_count,
):
    smem = pl.BlockSpec(memory_space=pltpu.SMEM)
    hbm = pl.BlockSpec(memory_space=pl.ANY)
    meta = functools.partial(pltpu.VMEM, dtype=jnp.int32)
    return pl.pallas_call(
        kernel,
        out_shape=jax.ShapeDtypeStruct((ROWS, OSLOT, BLK, BLK), jnp.float32),
        in_specs=[smem] * 6 + [hbm] * 2,
        out_specs=pl.BlockSpec(memory_space=pltpu.VMEM),
        scratch_shapes=[pltpu.VMEM((8, ROWS, LSLOT, BLK, BLK), jnp.bfloat16)]
        + [pltpu.VMEM((GROUP + 1, BLK, BLK), jnp.bfloat16)] * NZ
        + [
            meta((4, 8, BLK)),
            meta((8, BLK)),
            meta((NZ - 1, 8, BLK)),
            meta((2, 8, BLK)),
            meta((8, BLK)),
            meta((NX, 8, BLK)),
            meta((ROWS * OSLOT, 2 * BLK)),
            pltpu.SMEM((ROWS * OSLOT, 2 * BLK), jnp.int32),
            pltpu.SMEM((8, BLK), jnp.int32),
            pltpu.SemaphoreType.DMA((COPIES,)),
            pltpu.SemaphoreType.DMA((COPIES,)),
            pltpu.SemaphoreType.DMA((4,)),
        ],
        compiler_params=pltpu.CompilerParams(
            collective_id=0, has_side_effects=True, vmem_limit_bytes=48 * 1024 * 1024
        ),
    )(
        left_index,
        left_count,
        right_index,
        right_count,
        product_index,
        product_count,
        left_blocks,
        right_blocks.reshape(RDEV, BLK, BLK),
    )


def solution(mesh):
    return jax.shard_map(
        per_device,
        mesh=mesh,
        in_specs=(
            P("row", "col", None, None),
            P("row", "col"),
            P("row", "col"),
            P("row", "col", None, None),
            P("row", "col"),
            P("row", "col"),
            P("row", "col"),
            P("row", "col"),
        ),
        out_specs=P("row", "col", None, None),
        check_vma=False,
    )
```

```python
import functools

import jax
import jax.numpy as jnp
from jax import lax
from jax.experimental import pallas as pl
from jax.experimental.pallas import tpu as pltpu
from jax.sharding import PartitionSpec as P

MESH = pl.DeviceIdType.MESH
BLK = 128
NZ, NX = 8, 4
ROWS, LSLOT, RSLOT, OSLOT = 4, 8, 3, 6
RDEV = ROWS * RSLOT
ZERO = 4 * RDEV
GROUP = ZERO + 1
COPIES = 96


def kernel(*refs):
    small_in, (left, right, out, lbuf, early, mid, far), rest = refs[:6], refs[6:13], refs[13:]
    small, rest = rest[:6], rest[6:]
    lidx, lcnt, ridx, rcnt, pidx, pcnt = small
    rm, rs, rc, lm, ls, lc, code_v, code, lk, send, recv, local = rest
    row, col = lax.axis_index("row"), lax.axis_index("col")
    z, h, e = row // 4, (row // 2) % 2, row % 2
    x, y = col // 2, col % 2

    def zdev(d):
        return (((z + d) % NZ) * 4 + h * 2 + e, col)

    def xdev(d):
        return (row, ((x + d) % NX) * 2 + y)

    hdev = (z * 4 + (1 - h) * 2 + e, col)
    edev = (z * 4 + h * 2 + (1 - e), col)
    ydev = (row, x * 2 + (1 - y))

    barrier = pltpu.get_barrier_semaphore()
    partners = [zdev(1), zdev(-1), xdev(1), xdev(-1), hdev, edev, ydev]
    for dev in partners:
        pl.semaphore_signal(barrier, inc=1, device_id=dev, device_id_type=MESH)

    def rpart(d, hh, half=None):
        ref, group = (far, 0) if d in (4, -4) else (mid, (d + 3) // 6) if d in (3, -3) else (early, d + 2)
        first = group * GROUP + (hh * 2 + e) * RDEV
        if half is None:
            return ref.at[pl.ds(first, RDEV)]
        return ref.at[pl.ds(first + half * (RDEV // 2), RDEV // 2)]

    def lpart(dx, yy, half=None):
        at = ((x + dx) % NX) * 2 + yy
        if half is None:
            return lbuf.at[at]
        return lbuf.at[at, pl.ds(2 * half, 2)]

    loads = [pltpu.make_async_copy(a, b, local.at[n]) for n, (a, b) in enumerate(zip(small_in, small))]
    for load in loads:
        load.start()
    own_left = pltpu.make_async_copy(left, lpart(0, y), local.at[6])
    own_left.start()
    own_right = pltpu.make_async_copy(right, rpart(0, h), local.at[7])
    own_right.start()
    for load in loads:
        load.wait()

    sub = lax.broadcasted_iota(jnp.int32, (8, BLK), 0)
    lane = lax.broadcasted_iota(jnp.int32, (8, BLK), 1)
    table = jnp.zeros((8, BLK), jnp.int32)
    for j in range(ROWS):
        for t in range(RSLOT):
            value = jnp.where(t < rcnt[j], ridx[j, t] + 1, 0)
            table = jnp.where((sub == t) & (lane == row * ROWS + j), value, table)
    rm[0] = table
    table = jnp.zeros((8, BLK), jnp.int32)
    for i in range(ROWS):
        for s in range(LSLOT):
            value = jnp.where(s % 2 < lcnt[i, s // 2], (col * 4 + s // 2) * ROWS + lidx[i, s] + 1, 0)
            table = jnp.where((sub == i) & (lane == col * LSLOT + s), value, table)
    lm[0] = table

    pl.semaphore_wait(barrier, len(partners))

    copies = {}

    def push(name, src, dst, dev):
        n = len(copies)
        copy = pltpu.make_async_remote_copy(
            src_ref=src,
            dst_ref=dst,
            send_sem=send.at[n],
            recv_sem=recv.at[n],
            device_id=dev,
            device_id_type=MESH,
        )
        copy.start()
        copies[name] = copy

    def arrived(*names):
        for name in names:
            copies[name].wait_recv()

    def hop(d, hh, tag, half):
        arrived(f"r+{d}{tag}{half}", f"r-{d}{tag}{half}")
        if d < 3 or half == 0:
            push(f"r+{d + 1}{tag}{half}", rpart(-d, hh, half), rpart(-d - 1, hh, half), zdev(1))
        if d < 3 or half == 1:
            push(f"r-{d + 1}{tag}{half}", rpart(d, hh, half), rpart(d + 1, hh, half), zdev(-1))

    def share(d, hh, tag):
        push(f"e-{d}{tag}", rpart(-d, hh), rpart(-d, hh), edev)
        push(f"e+{d}{tag}", rpart(d, hh), rpart(d, hh), edev)

    push("ma", rm.at[0], rm.at[1], edev)
    push("na", lm.at[0], lm.at[1], ydev)
    for half in range(2):
        own = right.at[pl.ds(half * (RDEV // 2), RDEV // 2)]
        push(f"r+1o{half}", own, rpart(-1, h, half), zdev(1))
        push(f"r-1o{half}", own, rpart(1, h, half), zdev(-1))
    push("rh", right, rpart(0, h), hdev)
    push("l+1a", left.at[pl.ds(0, 2)], lpart(0, y, 0), xdev(1))
    push("l-1b", left.at[pl.ds(2, 2)], lpart(0, y, 1), xdev(-1))
    push("lya", left.at[pl.ds(0, 2)], lpart(0, y, 0), ydev)
    push("l+1b", left.at[pl.ds(2, 2)], lpart(0, y, 1), xdev(1))
    push("l-1a", left.at[pl.ds(0, 2)], lpart(0, y, 0), xdev(-1))
    push("lyb", left.at[pl.ds(2, 2)], lpart(0, y, 1), ydev)
    push("e0o", right, rpart(0, h), edev)

    out[...] = jnp.zeros_like(out)
    for ref, groups in ((early, 5), (mid, 2), (far, 1)):
        for group in range(groups):
            ref[group * GROUP + ZERO] = jnp.zeros((BLK, BLK), jnp.bfloat16)
    code_v[:, BLK:] = jnp.full((ROWS * OSLOT, BLK), ZERO, jnp.int32)
    arrived("ma", "na")
    rs[...] = rm[0] + rm[1]
    ls[...] = lm[0] + lm[1]
    push("mb", rs, rm.at[2], hdev)
    push("nb+1", ls, lc.at[0], xdev(1))
    push("nb-1", ls, lc.at[2], xdev(-1))

    hop(1, h, "o", 0)
    hop(1, h, "o", 1)
    share(1, h, "o")
    arrived("mb")
    rc[0] = rs[...] + rm[2]
    push("mc+1", rc.at[0], rc.at[7], zdev(1))
    push("mc-1", rc.at[0], rc.at[1], zdev(-1))
    arrived("rh")
    for half in range(2):
        push(f"r+1p{half}", rpart(0, 1 - h, half), rpart(-1, 1 - h, half), zdev(1))
        push(f"r-1p{half}", rpart(0, 1 - h, half), rpart(1, 1 - h, half), zdev(-1))
    push("e0p", rpart(0, 1 - h), rpart(0, 1 - h), edev)
    arrived("l+1a", "l-1b")
    push("b-1", lpart(1, y, 1), lpart(1, y, 1), ydev)
    hop(2, h, "o", 0)
    hop(2, h, "o", 1)
    share(2, h, "o")
    arrived("mc+1", "mc-1", "nb+1", "nb-1")
    push("mc+2", rc.at[7], rc.at[6], zdev(1))
    push("mc-2", rc.at[1], rc.at[2], zdev(-1))
    push("nb+2", lc.at[0], lc.at[1], xdev(1))
    arrived("lya")
    push("a+1", lpart(0, 1 - y, 0), lpart(0, 1 - y, 0), xdev(1))
    push("a-1", lpart(0, 1 - y, 0), lpart(0, 1 - y, 0), xdev(-1))
    hop(1, 1 - h, "p", 0)
    arrived("l+1b", "l-1a")
    push("l+2", lpart(-1, y, 0), lpart(-1, y, 0), xdev(1))
    push("l-2", lpart(1, y, 1), lpart(1, y, 1), xdev(-1))
    push("b+1", lpart(-1, y, 1), lpart(-1, y, 1), ydev)
    hop(1, 1 - h, "p", 1)
    share(1, 1 - h, "p")
    arrived("mc+2", "mc-2", "nb+2")
    push("mc+3", rc.at[6], rc.at[5], zdev(1))
    push("mc-3", rc.at[2], rc.at[3], zdev(-1))
    hop(3, h, "o", 0)
    hop(3, h, "o", 1)
    share(3, h, "o")
    arrived("mc+3", "mc-3")
    push("mc+4", rc.at[5], rc.at[4], zdev(1))
    arrived("a+1", "a-1")
    push("a+2", lpart(-1, 1 - y, 0), lpart(-1, 1 - y, 0), xdev(1))
    hop(2, 1 - h, "p", 0)
    hop(2, 1 - h, "p", 1)
    share(2, 1 - h, "p")
    arrived("lyb", "b-1")
    push("b-2", lpart(1, 1 - y, 1), lpart(1, 1 - y, 1), xdev(-1))

    arrived("mc+4")
    right_table = rc[0]
    for d in range(1, NZ):
        right_table = right_table + rc[d]
    left_table = ls[...]
    for d in range(NX - 1):
        left_table = left_table + lc[d]
    lc[NX - 1] = jnp.where(left_table == 0, BLK, left_table - 1)
    wide_sub = lax.broadcasted_iota(jnp.int32, (ROWS * OSLOT, BLK), 0)
    wide_lane = lax.broadcasted_iota(jnp.int32, (ROWS * OSLOT, BLK), 1)
    wanted = jnp.full((ROWS * OSLOT, BLK), -1, jnp.int32)
    for i in range(ROWS):
        for u in range(OSLOT):
            value = jnp.where(u < pcnt[i], pidx[i, u] + 1, -1)
            wanted = jnp.where(wide_sub == i * OSLOT + u, value, wanted)
    found = jnp.full((ROWS * OSLOT, BLK), ZERO, jnp.int32)
    for t in range(RSLOT):
        found = jnp.where(right_table[t : t + 1, :] == wanted, (wide_lane % 16) * RSLOT + t, found)
    code_v[:, :BLK] = found
    to_code = pltpu.make_async_copy(code_v, code, local.at[8])
    to_code.start()
    to_lk = pltpu.make_async_copy(lc.at[NX - 1], lk, local.at[9])
    to_lk.start()

    def multiply(ref, groups, d_of, rows_of):
        def one_group(j, carry):
            c = (z + d_of(j) + NZ) % NZ
            dx, dy = (c // 2 - x + NX) % NX, (c + y) % 2

            def one_row(i, carry):
                ks = [lk[i, c * LSLOT + s] for s in range(LSLOT)]
                lhs = jnp.concatenate([lbuf[c, i, s] for s in range(LSLOT)], axis=1)
                for u in range(0, OSLOT, 2):
                    rhs = jnp.concatenate(
                        [
                            jnp.concatenate(
                                [ref[j * GROUP + code[i * OSLOT + u + n, ks[s]]] for n in range(2)], axis=1
                            )
                            for s in range(LSLOT)
                        ],
                        axis=0,
                    )
                    part = jnp.dot(lhs, rhs, preferred_element_type=jnp.float32)
                    out[i, u] += part[:, :BLK]
                    out[i, u + 1] += part[:, BLK:]
                return carry

            first, last = rows_of(dx, dy)
            lax.fori_loop(first, last, one_row, 0)
            return carry

        lax.fori_loop(0, groups, one_group, 0)

    def early_d(j):
        return j - 2

    def mid_d(j):
        return 6 * j - 3

    def far_d(j):
        return 4

    def first_point(dx, dy):
        return jnp.where(dx == 2, 0, jnp.where((dx == 3) & (dy == 1), 2, 4))

    def second_point(dx, dy):
        return jnp.where((dx == 2) & (dy == 1), 0, 4)

    for tag in "op":
        arrived(f"e0{tag}")
        for d in range(1, 3):
            arrived(f"e-{d}{tag}", f"e+{d}{tag}")
    own_left.wait()
    own_right.wait()
    to_code.wait()
    to_lk.wait()
    multiply(early, 5, early_d, lambda dx, dy: (0, first_point(dx, dy)))

    arrived("r+4o0", "r-4o1")
    push("e4o", rpart(4, h), rpart(4, h), edev)
    hop(3, 1 - h, "p", 0)
    hop(3, 1 - h, "p", 1)
    share(3, 1 - h, "p")
    arrived("l+2", "l-2", "b+1")
    multiply(early, 5, early_d, lambda dx, dy: (first_point(dx, dy), second_point(dx, dy)))
    for tag in "op":
        arrived(f"e-3{tag}", f"e+3{tag}")
    multiply(mid, 2, mid_d, lambda dx, dy: (0, second_point(dx, dy)))
    arrived("r+4p0", "r-4p1")
    push("e4p", rpart(4, 1 - h), rpart(4, 1 - h), edev)
    arrived("a+2", "b-2")
    multiply(early, 5, early_d, lambda dx, dy: (second_point(dx, dy), 4))
    multiply(mid, 2, mid_d, lambda dx, dy: (second_point(dx, dy), 4))
    arrived("e4o", "e4p")
    multiply(far, 1, far_d, lambda dx, dy: (0, 4))

    for copy in copies.values():
        copy.wait_send()


def per_device(
    left_blocks,
    left_index,
    left_count,
    right_blocks,
    right_index,
    right_count,
    product_index,
    product_count,
):
    small = (
        left_index,
        left_count,
        right_index,
        right_count.reshape(ROWS),
        product_index,
        product_count.reshape(ROWS),
    )
    meta = functools.partial(pltpu.VMEM, dtype=jnp.int32)
    return pl.pallas_call(
        kernel,
        out_shape=jax.ShapeDtypeStruct((ROWS, OSLOT, BLK, BLK), jnp.float32),
        in_specs=[pl.BlockSpec(memory_space=pltpu.HBM)] * 8,
        out_specs=pl.BlockSpec(memory_space=pltpu.VMEM),
        scratch_shapes=[pltpu.VMEM((8, ROWS, LSLOT, BLK, BLK), jnp.bfloat16)]
        + [pltpu.VMEM((n * GROUP, BLK, BLK), jnp.bfloat16) for n in (5, 2, 1)]
        + [pltpu.SMEM(a.shape, jnp.int32) for a in small]
        + [
            meta((3, 8, BLK)),
            meta((8, BLK)),
            meta((NZ, 8, BLK)),
            meta((2, 8, BLK)),
            meta((8, BLK)),
            meta((NX, 8, BLK)),
            meta((ROWS * OSLOT, 2 * BLK)),
            pltpu.SMEM((ROWS * OSLOT, 2 * BLK), jnp.int32),
            pltpu.SMEM((8, BLK), jnp.int32),
            pltpu.SemaphoreType.DMA((COPIES,)),
            pltpu.SemaphoreType.DMA((COPIES,)),
            pltpu.SemaphoreType.DMA((10,)),
        ],
        compiler_params=pltpu.CompilerParams(
            collective_id=0, has_side_effects=True, vmem_limit_bytes=63 * 1024 * 1024
        ),
    )(*small, left_blocks, right_blocks.reshape(RDEV, BLK, BLK))


def solution(mesh):
    return jax.shard_map(
        per_device,
        mesh=mesh,
        in_specs=(
            P("row", "col", None, None),
            P("row", "col"),
            P("row", "col"),
            P("row", "col", None, None),
            P("row", "col"),
            P("row", "col"),
            P("row", "col"),
            P("row", "col"),
        ),
        out_specs=P("row", "col", None, None),
        check_vma=False,
    )
```

```python
import functools

import jax
import jax.numpy as jnp
from jax import lax
from jax.experimental import pallas as pl
from jax.experimental.pallas import tpu as pltpu
from jax.sharding import PartitionSpec as P

MESH = pl.DeviceIdType.MESH
BLK = 128
NZ, NX = 8, 4
ROWS, LSLOT, RSLOT, OSLOT = 4, 8, 3, 6
RDEV = ROWS * RSLOT
ZERO = 4 * RDEV
GROUP = ZERO + 1
COPIES = 96


def kernel(*refs):
    small_in, (left, right, out, lbuf, early, mid, far), rest = refs[:6], refs[6:13], refs[13:]
    small, rest = rest[:6], rest[6:]
    lidx, lcnt, ridx, rcnt, pidx, pcnt = small
    rm, rs, rc, lm, ls, lc, code_v, code, lk, send, recv, local = rest
    row, col = lax.axis_index("row"), lax.axis_index("col")
    z, h, e = row // 4, (row // 2) % 2, row % 2
    x, y = col // 2, col % 2

    def zdev(d):
        return (((z + d) % NZ) * 4 + h * 2 + e, col)

    def xdev(d):
        return (row, ((x + d) % NX) * 2 + y)

    hdev = (z * 4 + (1 - h) * 2 + e, col)
    edev = (z * 4 + h * 2 + (1 - e), col)
    ydev = (row, x * 2 + (1 - y))

    barrier = pltpu.get_barrier_semaphore()
    partners = [zdev(1), zdev(-1), xdev(1), xdev(-1), hdev, edev, ydev]
    for dev in partners:
        pl.semaphore_signal(barrier, inc=1, device_id=dev, device_id_type=MESH)

    def rpart(d, hh, half=None):
        ref, group = (far, 0) if d in (4, -4) else (mid, (d + 3) // 6) if d in (3, -3) else (early, d + 2)
        first = group * GROUP + (hh * 2 + e) * RDEV
        if half is None:
            return ref.at[pl.ds(first, RDEV)]
        return ref.at[pl.ds(first + half * (RDEV // 2), RDEV // 2)]

    def lpart(dx, yy, half=None):
        at = ((x + dx) % NX) * 2 + yy
        if half is None:
            return lbuf.at[at]
        return lbuf.at[at, pl.ds(2 * half, 2)]

    loads = [pltpu.make_async_copy(a, b, local.at[n]) for n, (a, b) in enumerate(zip(small_in, small))]
    for load in loads:
        load.start()
    own_left = pltpu.make_async_copy(left, lpart(0, y), local.at[6])
    own_left.start()
    own_right = pltpu.make_async_copy(right, rpart(0, h), local.at[7])
    own_right.start()
    for load in loads:
        load.wait()

    sub = lax.broadcasted_iota(jnp.int32, (8, BLK), 0)
    lane = lax.broadcasted_iota(jnp.int32, (8, BLK), 1)
    table = jnp.zeros((8, BLK), jnp.int32)
    for j in range(ROWS):
        for t in range(RSLOT):
            value = jnp.where(t < rcnt[j], ridx[j, t] + 1, 0)
            table = jnp.where((sub == t) & (lane == row * ROWS + j), value, table)
    rm[0] = table
    table = jnp.zeros((8, BLK), jnp.int32)
    for i in range(ROWS):
        for s in range(LSLOT):
            value = jnp.where(s % 2 < lcnt[i, s // 2], (col * 4 + s // 2) * ROWS + lidx[i, s] + 1, 0)
            table = jnp.where((sub == i) & (lane == col * LSLOT + s), value, table)
    lm[0] = table

    pl.semaphore_wait(barrier, len(partners))

    copies = {}

    def push(name, src, dst, dev):
        n = len(copies)
        copy = pltpu.make_async_remote_copy(
            src_ref=src,
            dst_ref=dst,
            send_sem=send.at[n],
            recv_sem=recv.at[n],
            device_id=dev,
            device_id_type=MESH,
        )
        copy.start()
        copies[name] = copy

    def arrived(*names):
        for name in names:
            copies[name].wait_recv()

    def hop(d, hh, tag, half):
        arrived(f"r+{d}{tag}{half}", f"r-{d}{tag}{half}")
        if d < 3 or half == 0:
            push(f"r+{d + 1}{tag}{half}", rpart(-d, hh, half), rpart(-d - 1, hh, half), zdev(1))
        if d < 3 or half == 1:
            push(f"r-{d + 1}{tag}{half}", rpart(d, hh, half), rpart(d + 1, hh, half), zdev(-1))

    def share(d, hh, tag):
        push(f"e-{d}{tag}", rpart(-d, hh), rpart(-d, hh), edev)
        push(f"e+{d}{tag}", rpart(d, hh), rpart(d, hh), edev)

    push("ma", rm.at[0], rm.at[1], edev)
    push("na", lm.at[0], lm.at[1], ydev)
    for half in range(2):
        own = right.at[pl.ds(half * (RDEV // 2), RDEV // 2)]
        push(f"r+1o{half}", own, rpart(-1, h, half), zdev(1))
        push(f"r-1o{half}", own, rpart(1, h, half), zdev(-1))
    arrived("ma", "na")
    rs[...] = rm[0] + rm[1]
    ls[...] = lm[0] + lm[1]
    push("mb", rs, rm.at[2], hdev)
    push("nb+1", ls, lc.at[0], xdev(1))
    push("nb-1", ls, lc.at[2], xdev(-1))
    push("rh", right, rpart(0, h), hdev)
    push("l+1a", left.at[pl.ds(0, 2)], lpart(0, y, 0), xdev(1))
    push("l-1b", left.at[pl.ds(2, 2)], lpart(0, y, 1), xdev(-1))
    push("lya", left.at[pl.ds(0, 2)], lpart(0, y, 0), ydev)
    push("e0o", right, rpart(0, h), edev)
    arrived("mb", "nb+1", "nb-1")
    rc[0] = rs[...] + rm[2]
    push("mc+1", rc.at[0], rc.at[7], zdev(1))
    push("mc-1", rc.at[0], rc.at[1], zdev(-1))
    push("nb+2", lc.at[0], lc.at[1], xdev(1))
    push("l+1b", left.at[pl.ds(2, 2)], lpart(0, y, 1), xdev(1))
    push("l-1a", left.at[pl.ds(0, 2)], lpart(0, y, 0), xdev(-1))
    push("lyb", left.at[pl.ds(2, 2)], lpart(0, y, 1), ydev)

    hop(1, h, "o", 0)
    out[...] = jnp.zeros_like(out)
    for ref, groups in ((early, 5), (mid, 2), (far, 1)):
        for group in range(groups):
            ref[group * GROUP + ZERO] = jnp.zeros((BLK, BLK), jnp.bfloat16)
    code_v[:, BLK:] = jnp.full((ROWS * OSLOT, BLK), ZERO, jnp.int32)
    arrived("mc+1", "mc-1")
    push("mc+2", rc.at[7], rc.at[6], zdev(1))
    push("mc-2", rc.at[1], rc.at[2], zdev(-1))
    hop(1, h, "o", 1)
    share(1, h, "o")
    arrived("rh")
    for half in range(2):
        push(f"r+1p{half}", rpart(0, 1 - h, half), rpart(-1, 1 - h, half), zdev(1))
        push(f"r-1p{half}", rpart(0, 1 - h, half), rpart(1, 1 - h, half), zdev(-1))
    push("e0p", rpart(0, 1 - h), rpart(0, 1 - h), edev)
    arrived("l+1a", "l-1b")
    push("b-1", lpart(1, y, 1), lpart(1, y, 1), ydev)
    arrived("mc+2", "mc-2")
    push("mc+3", rc.at[6], rc.at[5], zdev(1))
    push("mc-3", rc.at[2], rc.at[3], zdev(-1))
    hop(2, h, "o", 0)
    hop(2, h, "o", 1)
    share(2, h, "o")
    arrived("lya")
    push("a+1", lpart(0, 1 - y, 0), lpart(0, 1 - y, 0), xdev(1))
    push("a-1", lpart(0, 1 - y, 0), lpart(0, 1 - y, 0), xdev(-1))
    arrived("mc+3", "mc-3")
    push("mc+4", rc.at[5], rc.at[4], zdev(1))
    hop(1, 1 - h, "p", 0)
    arrived("l+1b", "l-1a")
    push("l+2", lpart(-1, y, 0), lpart(-1, y, 0), xdev(1))
    push("l-2", lpart(1, y, 1), lpart(1, y, 1), xdev(-1))
    push("b+1", lpart(-1, y, 1), lpart(-1, y, 1), ydev)
    hop(1, 1 - h, "p", 1)
    share(1, 1 - h, "p")
    hop(3, h, "o", 0)
    hop(3, h, "o", 1)
    share(3, h, "o")
    arrived("a+1", "a-1")
    push("a+2", lpart(-1, 1 - y, 0), lpart(-1, 1 - y, 0), xdev(1))
    hop(2, 1 - h, "p", 0)
    hop(2, 1 - h, "p", 1)
    share(2, 1 - h, "p")
    arrived("lyb", "b-1")
    push("b-2", lpart(1, 1 - y, 1), lpart(1, 1 - y, 1), xdev(-1))

    arrived("nb+2", "mc+4")
    right_table = rc[0]
    for d in range(1, NZ):
        right_table = right_table + rc[d]
    left_table = ls[...]
    for d in range(NX - 1):
        left_table = left_table + lc[d]
    lc[NX - 1] = jnp.where(left_table == 0, BLK, left_table - 1)
    wide_sub = lax.broadcasted_iota(jnp.int32, (ROWS * OSLOT, BLK), 0)
    wide_lane = lax.broadcasted_iota(jnp.int32, (ROWS * OSLOT, BLK), 1)
    wanted = jnp.full((ROWS * OSLOT, BLK), -1, jnp.int32)
    for i in range(ROWS):
        for u in range(OSLOT):
            value = jnp.where(u < pcnt[i], pidx[i, u] + 1, -1)
            wanted = jnp.where(wide_sub == i * OSLOT + u, value, wanted)
    found = jnp.full((ROWS * OSLOT, BLK), ZERO, jnp.int32)
    for t in range(RSLOT):
        found = jnp.where(right_table[t : t + 1, :] == wanted, (wide_lane % 16) * RSLOT + t, found)
    code_v[:, :BLK] = found
    to_code = pltpu.make_async_copy(code_v, code, local.at[8])
    to_code.start()
    to_lk = pltpu.make_async_copy(lc.at[NX - 1], lk, local.at[9])
    to_lk.start()

    def multiply(ref, groups, d_of, rows_of):
        def one_group(j, carry):
            c = (z + d_of(j) + NZ) % NZ
            dx, dy = (c // 2 - x + NX) % NX, (c + y) % 2

            def one_row(i, carry):
                ks = [lk[i, c * LSLOT + s] for s in range(LSLOT)]
                lhs = jnp.concatenate([lbuf[c, i, s] for s in range(LSLOT)], axis=1)
                for u in range(0, OSLOT, 2):
                    rhs = jnp.concatenate(
                        [
                            jnp.concatenate(
                                [ref[j * GROUP + code[i * OSLOT + u + n, ks[s]]] for n in range(2)], axis=1
                            )
                            for s in range(LSLOT)
                        ],
                        axis=0,
                    )
                    part = jnp.dot(lhs, rhs, preferred_element_type=jnp.float32)
                    out[i, u] += part[:, :BLK]
                    out[i, u + 1] += part[:, BLK:]
                return carry

            first, last = rows_of(dx, dy)
            lax.fori_loop(first, last, one_row, 0)
            return carry

        lax.fori_loop(0, groups, one_group, 0)

    def early_d(j):
        return j - 2

    def mid_d(j):
        return 6 * j - 3

    def far_d(j):
        return 4

    def first_point(dx, dy):
        return jnp.where(dx == 2, 0, jnp.where((dx == 3) & (dy == 1), 2, 4))

    def second_point(dx, dy):
        return jnp.where((dx == 2) & (dy == 1), 0, 4)

    for tag in "op":
        arrived(f"e0{tag}")
        for d in range(1, 3):
            arrived(f"e-{d}{tag}", f"e+{d}{tag}")
    own_left.wait()
    own_right.wait()
    to_code.wait()
    to_lk.wait()
    multiply(early, 5, early_d, lambda dx, dy: (0, first_point(dx, dy)))

    arrived("r+4o0", "r-4o1")
    push("e4o", rpart(4, h), rpart(4, h), edev)
    hop(3, 1 - h, "p", 0)
    hop(3, 1 - h, "p", 1)
    share(3, 1 - h, "p")
    arrived("l+2", "l-2", "b+1")
    multiply(early, 5, early_d, lambda dx, dy: (first_point(dx, dy), second_point(dx, dy)))
    for tag in "op":
        arrived(f"e-3{tag}", f"e+3{tag}")
    multiply(mid, 2, mid_d, lambda dx, dy: (0, second_point(dx, dy)))
    arrived("r+4p0", "r-4p1")
    push("e4p", rpart(4, 1 - h), rpart(4, 1 - h), edev)
    arrived("a+2", "b-2")
    multiply(early, 5, early_d, lambda dx, dy: (second_point(dx, dy), 4))
    multiply(mid, 2, mid_d, lambda dx, dy: (second_point(dx, dy), 4))
    arrived("e4o", "e4p")
    multiply(far, 1, far_d, lambda dx, dy: (0, 4))

    for copy in copies.values():
        copy.wait_send()


def per_device(
    left_blocks,
    left_index,
    left_count,
    right_blocks,
    right_index,
    right_count,
    product_index,
    product_count,
):
    small = (
        left_index,
        left_count,
        right_index,
        right_count.reshape(ROWS),
        product_index,
        product_count.reshape(ROWS),
    )
    meta = functools.partial(pltpu.VMEM, dtype=jnp.int32)
    return pl.pallas_call(
        kernel,
        out_shape=jax.ShapeDtypeStruct((ROWS, OSLOT, BLK, BLK), jnp.float32),
        in_specs=[pl.BlockSpec(memory_space=pltpu.HBM)] * 8,
        out_specs=pl.BlockSpec(memory_space=pltpu.VMEM),
        scratch_shapes=[pltpu.VMEM((8, ROWS, LSLOT, BLK, BLK), jnp.bfloat16)]
        + [pltpu.VMEM((n * GROUP, BLK, BLK), jnp.bfloat16) for n in (5, 2, 1)]
        + [pltpu.SMEM(a.shape, jnp.int32) for a in small]
        + [
            meta((3, 8, BLK)),
            meta((8, BLK)),
            meta((NZ, 8, BLK)),
            meta((2, 8, BLK)),
            meta((8, BLK)),
            meta((NX, 8, BLK)),
            meta((ROWS * OSLOT, 2 * BLK)),
            pltpu.SMEM((ROWS * OSLOT, 2 * BLK), jnp.int32),
            pltpu.SMEM((8, BLK), jnp.int32),
            pltpu.SemaphoreType.DMA((COPIES,)),
            pltpu.SemaphoreType.DMA((COPIES,)),
            pltpu.SemaphoreType.DMA((10,)),
        ],
        compiler_params=pltpu.CompilerParams(
            collective_id=0, has_side_effects=True, vmem_limit_bytes=63 * 1024 * 1024
        ),
    )(*small, left_blocks, right_blocks.reshape(RDEV, BLK, BLK))


def solution(mesh):
    return jax.shard_map(
        per_device,
        mesh=mesh,
        in_specs=(
            P("row", "col", None, None),
            P("row", "col"),
            P("row", "col"),
            P("row", "col", None, None),
            P("row", "col"),
            P("row", "col"),
            P("row", "col"),
            P("row", "col"),
        ),
        out_specs=P("row", "col", None, None),
        check_vma=False,
    )
```

```python
import functools

import jax
import jax.numpy as jnp
from jax import lax
from jax.experimental import pallas as pl
from jax.experimental.pallas import tpu as pltpu
from jax.sharding import PartitionSpec as P

MESH = pl.DeviceIdType.MESH
BLK = 128
NZ, NX = 8, 4
ROWS, LSLOT, RSLOT, OSLOT = 4, 8, 3, 6
RDEV = ROWS * RSLOT
ZERO = RDEV
PART = RDEV + 1
COPIES = 96


def kernel(*refs):
    small_in, (left, right, out, acc, lbuf), parts, rest = refs[:6], refs[6:11], refs[11:18], refs[18:]
    small, rest = rest[:6], rest[6:]
    near, next_, mid_o, mid_p, far_o, far_p, far_q = parts
    lidx, lcnt, ridx, rcnt, pidx, pcnt = small
    rm, rc, lm, ls, lc, code_v, code, lk, send, recv, local, done = rest
    row, col = lax.axis_index("row"), lax.axis_index("col")
    z, h, e = row // 4, (row // 2) % 2, row % 2
    x, y = col // 2, col % 2

    def zdev(d):
        return (((z + d) % NZ) * 4 + h * 2 + e, col)

    def xdev(d):
        return (row, ((x + d) % NX) * 2 + y)

    hdev = (z * 4 + (1 - h) * 2 + e, col)
    edev = (z * 4 + h * 2 + (1 - e), col)
    ydev = (row, x * 2 + (1 - y))

    barrier = pltpu.get_barrier_semaphore()
    partners = [zdev(1), zdev(-1), xdev(1), xdev(-1), hdev, edev, ydev]
    for dev in partners:
        pl.semaphore_signal(barrier, inc=1, device_id=dev, device_id_type=MESH)

    def rpart(d, tag, half=None):
        hh = h if tag == "o" else 1 - h
        if d in (-1, 0, 1):
            ref, at = near, (d + 1) * 4 + hh * 2 + e
        elif d in (-2, 2):
            ref, at = next_, (d + 2) + hh * 2 + e
        elif d in (-3, 3):
            ref, at = (mid_o if tag == "o" else mid_p), (d + 3) // 3 + e
        else:
            ref, at = (far_o, e) if tag == "o" else (far_p, 0)
        if half is None:
            return ref.at[pl.ds(at * PART, RDEV)]
        return ref.at[pl.ds(at * PART + half * (RDEV // 2), RDEV // 2)]

    def lpart(dx, yy, half=None):
        at = ((x + dx) % NX) * 2 + yy
        if half is None:
            return lbuf.at[at]
        return lbuf.at[at, pl.ds(2 * half, 2)]

    def lrow(dx, yy, i):
        return lbuf.at[((x + dx) % NX) * 2 + yy, pl.ds(i, 1)]

    loads = [pltpu.make_async_copy(a, b, local.at[n]) for n, (a, b) in enumerate(zip(small_in, small))]
    for load in loads:
        load.start()
    own_left = pltpu.make_async_copy(left, lpart(0, y), local.at[6])
    own_left.start()
    own_right = pltpu.make_async_copy(right, rpart(0, "o"), local.at[7])
    own_right.start()
    for load in loads:
        load.wait()

    sub = lax.broadcasted_iota(jnp.int32, (8, BLK), 0)
    lane = lax.broadcasted_iota(jnp.int32, (8, BLK), 1)
    table = jnp.zeros((8, BLK), jnp.int32)
    for j in range(ROWS):
        for t in range(RSLOT):
            value = jnp.where(t < rcnt[j], ridx[j, t] + 1, 0)
            table = jnp.where((sub == t) & (lane == row * ROWS + j), value, table)
    rm[0] = table
    table = jnp.zeros((8, BLK), jnp.int32)
    for i in range(ROWS):
        for s in range(LSLOT):
            value = jnp.where(s % 2 < lcnt[i, s // 2], (col * 4 + s // 2) * ROWS + lidx[i, s] + 1, 0)
            table = jnp.where((sub == i) & (lane == col * LSLOT + s), value, table)
    lm[0] = table

    pl.semaphore_wait(barrier, len(partners))

    copies = {}

    def push(name, src, dst, dev):
        n = len(copies)
        copy = pltpu.make_async_remote_copy(
            src_ref=src,
            dst_ref=dst,
            send_sem=send.at[n],
            recv_sem=recv.at[n],
            device_id=dev,
            device_id_type=MESH,
        )
        copy.start()
        copies[name] = copy

    def arrived(*names):
        for name in names:
            copies[name].wait_recv()

    def hop(d, tag, half):
        arrived(f"r+{d}{tag}{half}", f"r-{d}{tag}{half}")
        if d < 3 or half == 0:
            push(f"r+{d + 1}{tag}{half}", rpart(-d, tag, half), rpart(-d - 1, tag, half), zdev(1))
        if d < 3 or half == 1:
            push(f"r-{d + 1}{tag}{half}", rpart(d, tag, half), rpart(d + 1, tag, half), zdev(-1))

    def last(d, half):
        arrived(f"r+{d}p{half}", f"r-{d}p{half}")
        for n in range(2):
            at = pl.ds(6 * half + 3 * n, 3)
            way, below = ("-", 1) if half else ("+", -1)
            src = mid_p.at[pl.ds(((1 + below) + e) * PART + 6 * half + 3 * n, 3)]
            push(f"r{way}4p{n}", src, far_p.at[at], zdev(-below))

    def share(d, tag):
        push(f"e-{d}{tag}", rpart(-d, tag), rpart(-d, tag), edev)
        push(f"e+{d}{tag}", rpart(d, tag), rpart(d, tag), edev)

    def multiply(ref, d_of, devices, rows_of, write=False):
        groups = ref.shape[0] // (PART * len(devices))

        def one_group(j, carry):
            c = (z + d_of(j) + NZ) % NZ
            dx, dy = (c // 2 - x + NX) % NX, (c + y) % 2

            def one_row(i):
                slots = [(n, 2 * g + s) for n, g in enumerate(devices) for s in range(2)]
                ks = [lk[i, c * LSLOT + s] for _, s in slots]
                lhs = jnp.concatenate([lbuf[c, i, s] for _, s in slots], axis=1)
                for u in range(0, OSLOT, 2):
                    rhs = jnp.concatenate(
                        [
                            jnp.concatenate(
                                [
                                    ref[(j * len(devices) + n) * PART + code[i * OSLOT + u + v, k]]
                                    for v in range(2)
                                ],
                                axis=1,
                            )
                            for (n, _), k in zip(slots, ks)
                        ],
                        axis=0,
                    )
                    part = jnp.dot(lhs, rhs, preferred_element_type=jnp.float32)
                    acc[i, u] += part[:, :BLK]
                    acc[i, u + 1] += part[:, BLK:]
                if write:
                    pltpu.make_async_copy(acc.at[i], out.at[i], done.at[i]).start()

            def two_rows(i, carry):
                one_row(2 * i)
                one_row(2 * i + 1)
                return carry

            first, last = rows_of(dx, dy)
            lax.fori_loop(first // 2, last // 2, two_rows, 0)
            return carry

        if groups == 1:
            one_group(0, 0)
        else:
            lax.fori_loop(0, groups, one_group, 0)

    same, other, every = [h * 2, h * 2 + 1], [2 - h * 2, 3 - h * 2], range(4)
    products = {
        "near": (near, lambda j: j - 1, every),
        "next": (next_, lambda j: 4 * j - 2, every),
        "mid_o": (mid_o, lambda j: 6 * j - 3, same),
        "mid_p": (mid_p, lambda j: 6 * j - 3, other),
        "far_o": (far_o, lambda j: 4, same),
        "far_p": (far_p, lambda j: 4, [2 - h * 2 + e]),
        "far_q": (far_q, lambda j: 4, [3 - h * 2 - e]),
    }

    def rows_0(dx, dy):
        return jnp.where((dx != 2) & ((dy == 0) | (dx == 0)), 4, 0)

    def rows_2(dx, dy):
        return jnp.where(dy == 0, 4, jnp.where(dx == 2, 0, jnp.where(dx == 3, 2, 4)))

    def rows_3(dx, dy):
        return jnp.where((dx == 2) & (dy == 1), 0, 4)

    def nothing(dx, dy):
        return 0

    def everything(dx, dy):
        return 4

    def work(name, before, now, write=False):
        multiply(*products[name], lambda dx, dy: (before(dx, dy), now(dx, dy)), write)

    push("ma", rm.at[0], rm.at[1], edev)
    push("mh", rm.at[0], rm.at[2], hdev)
    push("na", lm.at[0], lm.at[1], ydev)
    for half in range(2):
        own = right.at[pl.ds(half * (RDEV // 2), RDEV // 2)]
        push(f"r+1o{half}", own, rpart(-1, "o", half), zdev(1))
        push(f"r-1o{half}", own, rpart(1, "o", half), zdev(-1))
    push("rh", right, rpart(0, "o"), hdev)
    push("l+1a", left.at[pl.ds(0, 2)], lpart(0, y, 0), xdev(1))
    push("l-1b", left.at[pl.ds(2, 2)], lpart(0, y, 1), xdev(-1))
    push("lya", left.at[pl.ds(0, 2)], lpart(0, y, 0), ydev)
    push("e0o", right, rpart(0, "o"), edev)
    arrived("mh")
    push("me", rm.at[2], rm.at[3], edev)
    arrived("na")
    ls[...] = lm[0] + lm[1]
    push("nb+1", ls, lc.at[0], xdev(1))
    push("nb-1", ls, lc.at[2], xdev(-1))
    push("l+1b", left.at[pl.ds(2, 2)], lpart(0, y, 1), xdev(1))
    push("l-1a", left.at[pl.ds(0, 2)], lpart(0, y, 0), xdev(-1))
    push("lyb", left.at[pl.ds(2, 2)], lpart(0, y, 1), ydev)
    arrived("ma", "me")
    rc[0] = rm[0] + rm[1] + rm[2] + rm[3]
    push("mc+1", rc.at[0], rc.at[7], zdev(1))
    push("mc-1", rc.at[0], rc.at[1], zdev(-1))

    hop(1, "o", 0)
    acc[...] = jnp.zeros_like(acc)
    for ref in parts:
        for n in range(ref.shape[0] // PART):
            ref[n * PART + ZERO] = jnp.zeros((BLK, BLK), jnp.bfloat16)
    code_v[:, BLK:] = jnp.full((ROWS * OSLOT, BLK), ZERO, jnp.int32)
    arrived("mc+1", "mc-1")
    push("mc+2", rc.at[7], rc.at[6], zdev(1))
    push("mc-2", rc.at[1], rc.at[2], zdev(-1))
    hop(1, "o", 1)
    share(1, "o")
    arrived("rh")
    for half in range(2):
        push(f"r+1p{half}", rpart(0, "p", half), rpart(-1, "p", half), zdev(1))
        push(f"r-1p{half}", rpart(0, "p", half), rpart(1, "p", half), zdev(-1))
    push("e0p", rpart(0, "p"), rpart(0, "p"), edev)
    arrived("mc+2", "mc-2")
    push("mc+3", rc.at[6], rc.at[5], zdev(1))
    push("mc-3", rc.at[2], rc.at[3], zdev(-1))
    hop(2, "o", 0)
    arrived("l+1a", "l-1b", "nb+1", "nb-1")
    push("nb+2", lc.at[0], lc.at[1], xdev(1))
    push("l+2", lpart(-1, y, 0), lpart(-1, y, 0), xdev(1))
    push("l-2", lpart(1, y, 1), lpart(1, y, 1), xdev(-1))
    push("b-1", lpart(1, y, 1), lpart(1, y, 1), ydev)
    hop(2, "o", 1)
    share(2, "o")
    arrived("mc+3", "mc-3")
    push("mc+4", rc.at[5], rc.at[4], zdev(1))
    hop(1, "p", 0)
    arrived("lya")
    for i in range(2):
        push(f"a+1{i}", lrow(0, 1 - y, i), lrow(0, 1 - y, i), xdev(1))
        push(f"a-1{i}", lrow(0, 1 - y, i), lrow(0, 1 - y, i), xdev(-1))
    arrived("l+1b", "l-1a")
    push("b+1", lpart(-1, y, 1), lpart(-1, y, 1), ydev)
    hop(1, "p", 1)
    share(1, "p")
    hop(3, "o", 0)
    arrived("nb+2", "mc+4")
    right_table = rc[0]
    for d in range(1, NZ):
        right_table = right_table + rc[d]
    left_table = ls[...]
    for d in range(NX - 1):
        left_table = left_table + lc[d]
    lc[NX - 1] = jnp.where(left_table == 0, BLK, left_table - 1)
    wide_sub = lax.broadcasted_iota(jnp.int32, (ROWS * OSLOT, BLK), 0)
    wide_lane = lax.broadcasted_iota(jnp.int32, (ROWS * OSLOT, BLK), 1)
    wanted = jnp.full((ROWS * OSLOT, BLK), -1, jnp.int32)
    for i in range(ROWS):
        for u in range(OSLOT):
            value = jnp.where(u < pcnt[i], pidx[i, u] + 1, -1)
            wanted = jnp.where(wide_sub == i * OSLOT + u, value, wanted)
    found = jnp.full((ROWS * OSLOT, BLK), ZERO, jnp.int32)
    for t in range(RSLOT):
        found = jnp.where(right_table[t : t + 1, :] == wanted, (wide_lane % ROWS) * RSLOT + t, found)
    code_v[:, :BLK] = found
    to_code = pltpu.make_async_copy(code_v, code, local.at[8])
    to_code.start()
    to_lk = pltpu.make_async_copy(lc.at[NX - 1], lk, local.at[9])
    to_lk.start()

    hop(3, "o", 1)
    share(3, "o")
    own_left.wait()
    own_right.wait()
    to_code.wait()
    to_lk.wait()
    for tag in "op":
        arrived(f"e0{tag}", f"e-1{tag}", f"e+1{tag}")
    arrived("lyb")
    work("near", nothing, rows_0)
    hop(2, "p", 0)
    arrived("a+10", "a-10")
    push("a+20", lrow(-1, 1 - y, 0), lrow(-1, 1 - y, 0), xdev(1))
    hop(2, "p", 1)
    share(2, "p")
    arrived("b-1")
    push("b-2", lpart(1, 1 - y, 1), lpart(1, 1 - y, 1), xdev(-1))
    for tag in "op":
        arrived(f"e-2{tag}", f"e+2{tag}")
    work("next", nothing, rows_0)
    arrived("a+11", "a-11")
    push("a+21", lrow(-1, 1 - y, 1), lrow(-1, 1 - y, 1), xdev(1))
    arrived("r+4o0", "r-4o1")
    push("e4o", rpart(4, "o"), rpart(4, "o"), edev)
    arrived("l+2", "l-2", "e-3o", "e+3o")
    work("near", rows_0, rows_2)
    work("next", rows_0, rows_2)
    last(3, 0)
    work("mid_o", nothing, rows_2)
    last(3, 1)
    share(3, "p")
    arrived("b+1", "e4o")
    for name in ("near", "next", "mid_o", "far_o"):
        work(name, rows_2 if name != "far_o" else nothing, rows_3)
    arrived("a+20", "a+21", "b-2")
    for name in ("near", "next", "mid_o", "far_o"):
        work(name, rows_3, everything)
    arrived("e-3p", "e+3p")
    work("mid_p", nothing, everything)
    arrived("r+4p0", "r-4p0")
    push("e4p0", far_p.at[pl.ds(0, 3)], far_q.at[pl.ds(0, 3)], edev)
    push("e4p1", far_p.at[pl.ds(6, 3)], far_q.at[pl.ds(6, 3)], edev)
    arrived("r+4p1", "r-4p1")
    push("e4p2", far_p.at[pl.ds(3, 3)], far_q.at[pl.ds(3, 3)], edev)
    push("e4p3", far_p.at[pl.ds(9, 3)], far_q.at[pl.ds(9, 3)], edev)
    work("far_p", nothing, everything)
    arrived("e4p0", "e4p1", "e4p2", "e4p3")
    work("far_q", nothing, everything, write=True)

    for copy in copies.values():
        copy.wait_send()
    for i in range(ROWS):
        pltpu.make_async_copy(acc.at[i], out.at[i], done.at[i]).wait()


def per_device(
    left_blocks,
    left_index,
    left_count,
    right_blocks,
    right_index,
    right_count,
    product_index,
    product_count,
):
    small = (
        left_index,
        left_count,
        right_index,
        right_count.reshape(ROWS),
        product_index,
        product_count.reshape(ROWS),
    )
    meta = functools.partial(pltpu.VMEM, dtype=jnp.int32)
    return pl.pallas_call(
        kernel,
        out_shape=jax.ShapeDtypeStruct((ROWS, OSLOT, BLK, BLK), jnp.float32),
        in_specs=[pl.BlockSpec(memory_space=pltpu.HBM)] * 8,
        out_specs=pl.BlockSpec(memory_space=pl.ANY),
        scratch_shapes=[
            pltpu.VMEM((ROWS, OSLOT, BLK, BLK), jnp.float32),
            pltpu.VMEM((8, ROWS, LSLOT, BLK, BLK), jnp.bfloat16),
        ]
        + [pltpu.VMEM((n * PART, BLK, BLK), jnp.bfloat16) for n in (12, 8, 4, 4, 2, 1, 1)]
        + [pltpu.SMEM(a.shape, jnp.int32) for a in small]
        + [
            meta((4, 8, BLK)),
            meta((NZ, 8, BLK)),
            meta((2, 8, BLK)),
            meta((8, BLK)),
            meta((NX, 8, BLK)),
            meta((ROWS * OSLOT, 2 * BLK)),
            pltpu.SMEM((ROWS * OSLOT, 2 * BLK), jnp.int32),
            pltpu.SMEM((8, BLK), jnp.int32),
            pltpu.SemaphoreType.DMA((COPIES,)),
            pltpu.SemaphoreType.DMA((COPIES,)),
            pltpu.SemaphoreType.DMA((10,)),
            pltpu.SemaphoreType.DMA((ROWS,)),
        ],
        compiler_params=pltpu.CompilerParams(
            collective_id=0, has_side_effects=True, vmem_limit_bytes=63 * 1024 * 1024
        ),
    )(*small, left_blocks, right_blocks.reshape(RDEV, BLK, BLK))


def solution(mesh):
    return jax.shard_map(
        per_device,
        mesh=mesh,
        in_specs=(
            P("row", "col", None, None),
            P("row", "col"),
            P("row", "col"),
            P("row", "col", None, None),
            P("row", "col"),
            P("row", "col"),
            P("row", "col"),
            P("row", "col"),
        ),
        out_specs=P("row", "col", None, None),
        check_vma=False,
    )
```

```python
import functools

import jax
import jax.numpy as jnp
from jax import lax
from jax.experimental import pallas as pl
from jax.experimental.pallas import tpu as pltpu
from jax.sharding import PartitionSpec as P

MESH = pl.DeviceIdType.MESH
BLK = 128
NZ, NX = 8, 4
ROWS, LSLOT, RSLOT, OSLOT = 4, 8, 3, 6
RDEV = ROWS * RSLOT
ZERO = RDEV
PART = RDEV + 1
COPIES = 96


def kernel(*refs):
    small_in, (left, right, acc, lbuf), parts, rest = refs[:6], refs[6:10], refs[10:17], refs[17:]
    small, rest = rest[:6], rest[6:]
    near, next_, mid_o, mid_p, far_o, far_p, far_q = parts
    lidx, lcnt, ridx, rcnt, pidx, pcnt = small
    rm, rc, lm, ls, lc, code_v, code, lk, send, recv, local = rest
    row, col = lax.axis_index("row"), lax.axis_index("col")
    z, h, e = row // 4, (row // 2) % 2, row % 2
    x, y = col // 2, col % 2

    def zdev(d):
        return (((z + d) % NZ) * 4 + h * 2 + e, col)

    def xdev(d):
        return (row, ((x + d) % NX) * 2 + y)

    hdev = (z * 4 + (1 - h) * 2 + e, col)
    edev = (z * 4 + h * 2 + (1 - e), col)
    ydev = (row, x * 2 + (1 - y))

    barrier = pltpu.get_barrier_semaphore()
    partners = [zdev(1), zdev(-1), xdev(1), xdev(-1), hdev, edev, ydev]
    for dev in partners:
        pl.semaphore_signal(barrier, inc=1, device_id=dev, device_id_type=MESH)

    def rpart(d, tag, half=None):
        hh = h if tag == "o" else 1 - h
        if d in (-1, 0, 1):
            ref, at = near, (d + 1) * 4 + hh * 2 + e
        elif d in (-2, 2):
            ref, at = next_, (d + 2) + hh * 2 + e
        elif d in (-3, 3):
            ref, at = (mid_o if tag == "o" else mid_p), (d + 3) // 3 + e
        else:
            ref, at = (far_o, e) if tag == "o" else (far_p, 0)
        if half is None:
            return ref.at[pl.ds(at * PART, RDEV)]
        return ref.at[pl.ds(at * PART + half * (RDEV // 2), RDEV // 2)]

    def lpart(dx, yy, half=None):
        at = ((x + dx) % NX) * 2 + yy
        if half is None:
            return lbuf.at[at]
        return lbuf.at[at, pl.ds(2 * half, 2)]

    def lrow(dx, yy, i):
        return lbuf.at[((x + dx) % NX) * 2 + yy, pl.ds(i, 1)]

    loads = [pltpu.make_async_copy(a, b, local.at[n]) for n, (a, b) in enumerate(zip(small_in, small))]
    for load in loads:
        load.start()
    own_left = pltpu.make_async_copy(left, lpart(0, y), local.at[6])
    own_left.start()
    own_right = pltpu.make_async_copy(right, rpart(0, "o"), local.at[7])
    own_right.start()
    for load in loads:
        load.wait()

    sub = lax.broadcasted_iota(jnp.int32, (8, BLK), 0)
    lane = lax.broadcasted_iota(jnp.int32, (8, BLK), 1)
    table = jnp.zeros((8, BLK), jnp.int32)
    for j in range(ROWS):
        for t in range(RSLOT):
            value = jnp.where(t < rcnt[j], ridx[j, t] + 1, 0)
            table = jnp.where((sub == t) & (lane == row * ROWS + j), value, table)
    rm[0] = table
    table = jnp.zeros((8, BLK), jnp.int32)
    for i in range(ROWS):
        for s in range(LSLOT):
            value = jnp.where(s % 2 < lcnt[i, s // 2], (col * 4 + s // 2) * ROWS + lidx[i, s] + 1, 0)
            table = jnp.where((sub == i) & (lane == col * LSLOT + s), value, table)
    lm[0] = table

    pl.semaphore_wait(barrier, len(partners))

    copies = {}

    def push(name, src, dst, dev):
        n = len(copies)
        copy = pltpu.make_async_remote_copy(
            src_ref=src,
            dst_ref=dst,
            send_sem=send.at[n],
            recv_sem=recv.at[n],
            device_id=dev,
            device_id_type=MESH,
        )
        copy.start()
        copies[name] = copy

    def arrived(*names):
        for name in names:
            copies[name].wait_recv()

    def hop(d, tag, half):
        arrived(f"r+{d}{tag}{half}", f"r-{d}{tag}{half}")
        if d < 3 or half == 0:
            push(f"r+{d + 1}{tag}{half}", rpart(-d, tag, half), rpart(-d - 1, tag, half), zdev(1))
        if d < 3 or half == 1:
            push(f"r-{d + 1}{tag}{half}", rpart(d, tag, half), rpart(d + 1, tag, half), zdev(-1))

    def last(d, half):
        arrived(f"r+{d}p{half}", f"r-{d}p{half}")
        for n in range(2):
            at = pl.ds(6 * half + 3 * n, 3)
            way, below = ("-", 1) if half else ("+", -1)
            src = mid_p.at[pl.ds(((1 + below) + e) * PART + 6 * half + 3 * n, 3)]
            push(f"r{way}4p{n}", src, far_p.at[at], zdev(-below))

    def share(d, tag):
        push(f"e-{d}{tag}", rpart(-d, tag), rpart(-d, tag), edev)
        push(f"e+{d}{tag}", rpart(d, tag), rpart(d, tag), edev)

    def multiply(ref, d_of, devices, rows_of):
        groups = ref.shape[0] // (PART * len(devices))

        def one_group(j, carry):
            c = (z + d_of(j) + NZ) % NZ
            dx, dy = (c // 2 - x + NX) % NX, (c + y) % 2

            def one_row(i):
                slots = [(n, 2 * g + s) for n, g in enumerate(devices) for s in range(2)]
                ks = [lk[i, c * LSLOT + s] for _, s in slots]
                lhs = jnp.concatenate([lbuf[c, i, s] for _, s in slots], axis=1)
                for u in range(0, OSLOT, 2):
                    rhs = jnp.concatenate(
                        [
                            jnp.concatenate(
                                [
                                    ref[(j * len(devices) + n) * PART + code[i * OSLOT + u + v, k]]
                                    for v in range(2)
                                ],
                                axis=1,
                            )
                            for (n, _), k in zip(slots, ks)
                        ],
                        axis=0,
                    )
                    part = jnp.dot(lhs, rhs, preferred_element_type=jnp.float32)
                    acc[i, u] += part[:, :BLK]
                    acc[i, u + 1] += part[:, BLK:]

            def two_rows(i, carry):
                one_row(2 * i)
                one_row(2 * i + 1)
                return carry

            first, last = rows_of(dx, dy)
            lax.fori_loop(first // 2, last // 2, two_rows, 0)
            return carry

        if groups == 1:
            one_group(0, 0)
        else:
            lax.fori_loop(0, groups, one_group, 0)

    same, other, every = [h * 2, h * 2 + 1], [2 - h * 2, 3 - h * 2], range(4)
    products = {
        "near": (near, lambda j: j - 1, every),
        "next": (next_, lambda j: 4 * j - 2, every),
        "mid_o": (mid_o, lambda j: 6 * j - 3, same),
        "mid_p": (mid_p, lambda j: 6 * j - 3, other),
        "far_o": (far_o, lambda j: 4, same),
        "far_p": (far_p, lambda j: 4, [2 - h * 2 + e]),
        "far_q": (far_q, lambda j: 4, [3 - h * 2 - e]),
    }

    def rows_0(dx, dy):
        return jnp.where((dx != 2) & ((dy == 0) | (dx == 0)), 4, 0)

    def rows_2(dx, dy):
        return jnp.where(dy == 0, 4, jnp.where(dx == 2, 0, jnp.where(dx == 3, 2, 4)))

    def rows_3(dx, dy):
        return jnp.where((dx == 2) & (dy == 1), 0, 4)

    def nothing(dx, dy):
        return 0

    def everything(dx, dy):
        return 4

    def work(name, before, now):
        multiply(*products[name], lambda dx, dy: (before(dx, dy), now(dx, dy)))

    push("ma", rm.at[0], rm.at[1], edev)
    push("mh", rm.at[0], rm.at[2], hdev)
    push("na", lm.at[0], lm.at[1], ydev)
    for half in range(2):
        own = right.at[pl.ds(half * (RDEV // 2), RDEV // 2)]
        push(f"r+1o{half}", own, rpart(-1, "o", half), zdev(1))
        push(f"r-1o{half}", own, rpart(1, "o", half), zdev(-1))
    push("rh", right, rpart(0, "o"), hdev)
    push("l+1a", left.at[pl.ds(0, 2)], lpart(0, y, 0), xdev(1))
    push("l-1b", left.at[pl.ds(2, 2)], lpart(0, y, 1), xdev(-1))
    push("lya", left.at[pl.ds(0, 2)], lpart(0, y, 0), ydev)
    push("e0o", right, rpart(0, "o"), edev)
    arrived("mh")
    push("me", rm.at[2], rm.at[3], edev)
    arrived("na")
    ls[...] = lm[0] + lm[1]
    push("nb+1", ls, lc.at[0], xdev(1))
    push("nb-1", ls, lc.at[2], xdev(-1))
    push("l+1b", left.at[pl.ds(2, 2)], lpart(0, y, 1), xdev(1))
    push("l-1a", left.at[pl.ds(0, 2)], lpart(0, y, 0), xdev(-1))
    push("lyb", left.at[pl.ds(2, 2)], lpart(0, y, 1), ydev)
    arrived("ma", "me")
    rc[0] = rm[0] + rm[1] + rm[2] + rm[3]
    push("mc+1", rc.at[0], rc.at[7], zdev(1))
    push("mc-1", rc.at[0], rc.at[1], zdev(-1))

    hop(1, "o", 0)
    acc[...] = jnp.zeros_like(acc)
    for ref in parts:
        for n in range(ref.shape[0] // PART):
            ref[n * PART + ZERO] = jnp.zeros((BLK, BLK), jnp.bfloat16)
    code_v[:, BLK:] = jnp.full((ROWS * OSLOT, BLK), ZERO, jnp.int32)
    arrived("mc+1", "mc-1")
    push("mc+2", rc.at[7], rc.at[6], zdev(1))
    push("mc-2", rc.at[1], rc.at[2], zdev(-1))
    hop(1, "o", 1)
    share(1, "o")
    arrived("rh")
    for half in range(2):
        push(f"r+1p{half}", rpart(0, "p", half), rpart(-1, "p", half), zdev(1))
        push(f"r-1p{half}", rpart(0, "p", half), rpart(1, "p", half), zdev(-1))
    push("e0p", rpart(0, "p"), rpart(0, "p"), edev)
    arrived("mc+2", "mc-2")
    push("mc+3", rc.at[6], rc.at[5], zdev(1))
    push("mc-3", rc.at[2], rc.at[3], zdev(-1))
    hop(2, "o", 0)
    arrived("l+1a", "l-1b", "nb+1", "nb-1")
    push("nb+2", lc.at[0], lc.at[1], xdev(1))
    push("l+2", lpart(-1, y, 0), lpart(-1, y, 0), xdev(1))
    push("l-2", lpart(1, y, 1), lpart(1, y, 1), xdev(-1))
    push("b-1", lpart(1, y, 1), lpart(1, y, 1), ydev)
    hop(2, "o", 1)
    share(2, "o")
    arrived("mc+3", "mc-3")
    push("mc+4", rc.at[5], rc.at[4], zdev(1))
    hop(1, "p", 0)
    arrived("lya")
    for i in range(2):
        push(f"a+1{i}", lrow(0, 1 - y, i), lrow(0, 1 - y, i), xdev(1))
        push(f"a-1{i}", lrow(0, 1 - y, i), lrow(0, 1 - y, i), xdev(-1))
    arrived("l+1b", "l-1a")
    push("b+1", lpart(-1, y, 1), lpart(-1, y, 1), ydev)
    hop(1, "p", 1)
    share(1, "p")
    hop(3, "o", 0)
    arrived("nb+2", "mc+4")
    right_table = rc[0]
    for d in range(1, NZ):
        right_table = right_table + rc[d]
    left_table = ls[...]
    for d in range(NX - 1):
        left_table = left_table + lc[d]
    lc[NX - 1] = jnp.where(left_table == 0, BLK, left_table - 1)
    wide_sub = lax.broadcasted_iota(jnp.int32, (ROWS * OSLOT, BLK), 0)
    wide_lane = lax.broadcasted_iota(jnp.int32, (ROWS * OSLOT, BLK), 1)
    wanted = jnp.full((ROWS * OSLOT, BLK), -1, jnp.int32)
    for i in range(ROWS):
        for u in range(OSLOT):
            value = jnp.where(u < pcnt[i], pidx[i, u] + 1, -1)
            wanted = jnp.where(wide_sub == i * OSLOT + u, value, wanted)
    found = jnp.full((ROWS * OSLOT, BLK), ZERO, jnp.int32)
    for t in range(RSLOT):
        found = jnp.where(right_table[t : t + 1, :] == wanted, (wide_lane % ROWS) * RSLOT + t, found)
    code_v[:, :BLK] = found
    to_code = pltpu.make_async_copy(code_v, code, local.at[8])
    to_code.start()
    to_lk = pltpu.make_async_copy(lc.at[NX - 1], lk, local.at[9])
    to_lk.start()

    hop(3, "o", 1)
    share(3, "o")
    own_left.wait()
    own_right.wait()
    to_code.wait()
    to_lk.wait()
    for tag in "op":
        arrived(f"e0{tag}", f"e-1{tag}", f"e+1{tag}")
    arrived("lyb")
    work("near", nothing, rows_0)
    hop(2, "p", 0)
    arrived("a+10", "a-10")
    push("a+20", lrow(-1, 1 - y, 0), lrow(-1, 1 - y, 0), xdev(1))
    hop(2, "p", 1)
    share(2, "p")
    arrived("b-1")
    push("b-2", lpart(1, 1 - y, 1), lpart(1, 1 - y, 1), xdev(-1))
    for tag in "op":
        arrived(f"e-2{tag}", f"e+2{tag}")
    work("next", nothing, rows_0)
    arrived("a+11", "a-11")
    push("a+21", lrow(-1, 1 - y, 1), lrow(-1, 1 - y, 1), xdev(1))
    arrived("r+4o0", "r-4o1")
    push("e4o", rpart(4, "o"), rpart(4, "o"), edev)
    arrived("l+2", "l-2", "e-3o", "e+3o")
    work("near", rows_0, rows_2)
    work("next", rows_0, rows_2)
    last(3, 0)
    work("mid_o", nothing, rows_2)
    last(3, 1)
    share(3, "p")
    arrived("b+1", "e4o")
    for name in ("near", "next", "mid_o", "far_o"):
        work(name, rows_2 if name != "far_o" else nothing, rows_3)
    arrived("a+20", "a+21", "b-2")
    for name in ("near", "next", "mid_o", "far_o"):
        work(name, rows_3, everything)
    arrived("e-3p", "e+3p")
    work("mid_p", nothing, everything)
    arrived("r+4p0", "r-4p0")
    push("e4p0", far_p.at[pl.ds(0, 3)], far_q.at[pl.ds(0, 3)], edev)
    push("e4p1", far_p.at[pl.ds(6, 3)], far_q.at[pl.ds(6, 3)], edev)
    arrived("r+4p1", "r-4p1")
    push("e4p2", far_p.at[pl.ds(3, 3)], far_q.at[pl.ds(3, 3)], edev)
    push("e4p3", far_p.at[pl.ds(9, 3)], far_q.at[pl.ds(9, 3)], edev)
    work("far_p", nothing, everything)
    arrived("e4p0", "e4p1", "e4p2", "e4p3")
    work("far_q", nothing, everything)

    for copy in copies.values():
        copy.wait_send()


def per_device(
    left_blocks,
    left_index,
    left_count,
    right_blocks,
    right_index,
    right_count,
    product_index,
    product_count,
):
    small = (
        left_index,
        left_count,
        right_index,
        right_count.reshape(ROWS),
        product_index,
        product_count.reshape(ROWS),
    )
    operands = (*small, left_blocks, right_blocks.reshape(RDEV, BLK, BLK))
    meta = functools.partial(pltpu.VMEM, dtype=jnp.int32)
    return pl.pallas_call(
        kernel,
        out_shape=pltpu.VMEM((ROWS, OSLOT, BLK, BLK), jnp.float32),
        in_specs=[pl.BlockSpec(memory_space=pl.ANY)] * 8,
        out_specs=pl.BlockSpec(memory_space=pltpu.VMEM),
        scratch_shapes=[
            pltpu.VMEM((8, ROWS, LSLOT, BLK, BLK), jnp.bfloat16),
        ]
        + [pltpu.VMEM((n * PART, BLK, BLK), jnp.bfloat16) for n in (12, 8, 4, 4, 2, 1, 1)]
        + [pltpu.SMEM(a.shape, jnp.int32) for a in small]
        + [
            meta((4, 8, BLK)),
            meta((NZ, 8, BLK)),
            meta((2, 8, BLK)),
            meta((8, BLK)),
            meta((NX, 8, BLK)),
            meta((ROWS * OSLOT, 2 * BLK)),
            pltpu.SMEM((ROWS * OSLOT, 2 * BLK), jnp.int32),
            pltpu.SMEM((8, BLK), jnp.int32),
            pltpu.SemaphoreType.DMA((COPIES,)),
            pltpu.SemaphoreType.DMA((COPIES,)),
            pltpu.SemaphoreType.DMA((10,)),
        ],
        compiler_params=pltpu.CompilerParams(
            collective_id=0, has_side_effects=True, vmem_limit_bytes=48 * 1024 * 1024
        ),
    )(*[pltpu.with_memory_space_constraint(a, pltpu.HBM) for a in operands])


def solution(mesh):
    return jax.shard_map(
        per_device,
        mesh=mesh,
        in_specs=(
            P("row", "col", None, None),
            P("row", "col"),
            P("row", "col"),
            P("row", "col", None, None),
            P("row", "col"),
            P("row", "col"),
            P("row", "col"),
            P("row", "col"),
        ),
        out_specs=P("row", "col", None, None),
        check_vma=False,
    )
```

```python
import functools

import jax
import jax.numpy as jnp
from jax import lax
from jax.experimental import pallas as pl
from jax.experimental.pallas import tpu as pltpu
from jax.sharding import PartitionSpec as P

MESH = pl.DeviceIdType.MESH
BLK = 128
NZ, NX = 8, 4
ROWS, LSLOT, RSLOT, OSLOT = 4, 8, 3, 6
RDEV = ROWS * RSLOT
ZERO = RDEV
PART = RDEV + 1
COPIES = 96
TAIL = 2


def kernel(*refs):
    small_in, (left, right, acc, lbuf), parts, rest = refs[:6], refs[6:10], refs[10:17], refs[17:]
    small, rest = rest[:6], rest[6:]
    near, next_, mid_o, mid_p, far_o, far_p, far_q = parts
    lidx, lcnt, ridx, rcnt, pidx, pcnt = small
    rm, rc, lm, ls, lc, code_v, code, lk, send, recv, local = rest
    row, col = lax.axis_index("row"), lax.axis_index("col")
    z, h, e = row // 4, (row // 2) % 2, row % 2
    x, y = col // 2, col % 2

    def zdev(d):
        return (((z + d) % NZ) * 4 + h * 2 + e, col)

    def xdev(d):
        return (row, ((x + d) % NX) * 2 + y)

    hdev = (z * 4 + (1 - h) * 2 + e, col)
    edev = (z * 4 + h * 2 + (1 - e), col)
    ydev = (row, x * 2 + (1 - y))

    barrier = pltpu.get_barrier_semaphore()
    partners = [zdev(1), zdev(-1), xdev(1), xdev(-1), hdev, edev, ydev]
    for dev in partners:
        pl.semaphore_signal(barrier, inc=1, device_id=dev, device_id_type=MESH)

    def rpart(d, tag, half=None):
        hh = h if tag == "o" else 1 - h
        if d in (-1, 0, 1):
            ref, at = near, (d + 1) * 4 + hh * 2 + e
        elif d in (-2, 2):
            ref, at = next_, (d + 2) + hh * 2 + e
        elif d in (-3, 3):
            ref, at = (mid_o if tag == "o" else mid_p), (d + 3) // 3 + e
        else:
            ref, at = (far_o, e) if tag == "o" else (far_p, 0)
        if half is None:
            return ref.at[pl.ds(at * PART, RDEV)]
        return ref.at[pl.ds(at * PART + half * (RDEV // 2), RDEV // 2)]

    def rtail(d, tag):
        hh = h if tag == "o" else 1 - h
        return near.at[pl.ds(((d + 1) * 4 + hh * 2 + e) * PART + RDEV - TAIL, TAIL)]

    def rmost(d, half):
        first = ((d + 1) * 4 + (1 - h) * 2 + e) * PART + half * (RDEV // 2)
        return near.at[pl.ds(first, RDEV // 2 - half * TAIL)]

    def lpart(dx, yy, half=None):
        at = ((x + dx) % NX) * 2 + yy
        if half is None:
            return lbuf.at[at]
        return lbuf.at[at, pl.ds(2 * half, 2)]

    def lrow(dx, yy, i):
        return lbuf.at[((x + dx) % NX) * 2 + yy, pl.ds(i, 1)]

    loads = [pltpu.make_async_copy(a, b, local.at[n]) for n, (a, b) in enumerate(zip(small_in, small))]
    for load in loads:
        load.start()
    own_left = pltpu.make_async_copy(left, lpart(0, y), local.at[6])
    own_left.start()
    own_right = pltpu.make_async_copy(right, rpart(0, "o"), local.at[7])
    own_right.start()
    for load in loads:
        load.wait()

    sub = lax.broadcasted_iota(jnp.int32, (8, BLK), 0)
    lane = lax.broadcasted_iota(jnp.int32, (8, BLK), 1)
    table = jnp.zeros((8, BLK), jnp.int32)
    for j in range(ROWS):
        for t in range(RSLOT):
            value = jnp.where(t < rcnt[j], ridx[j, t] + 1, 0)
            table = jnp.where((sub == t) & (lane == row * ROWS + j), value, table)
    rm[0] = table
    table = jnp.zeros((8, BLK), jnp.int32)
    for i in range(ROWS):
        for s in range(LSLOT):
            value = jnp.where(s % 2 < lcnt[i, s // 2], (col * 4 + s // 2) * ROWS + lidx[i, s] + 1, 0)
            table = jnp.where((sub == i) & (lane == col * LSLOT + s), value, table)
    lm[0] = table

    pl.semaphore_wait(barrier, len(partners))

    copies = {}

    def push(name, src, dst, dev):
        n = len(copies)
        copy = pltpu.make_async_remote_copy(
            src_ref=src,
            dst_ref=dst,
            send_sem=send.at[n],
            recv_sem=recv.at[n],
            device_id=dev,
            device_id_type=MESH,
        )
        copy.start()
        copies[name] = copy

    def arrived(*names):
        for name in names:
            copies[name].wait_recv()

    def hop(d, tag, half):
        arrived(f"r+{d}{tag}{half}", f"r-{d}{tag}{half}")
        if d < 3 or half == 0:
            push(f"r+{d + 1}{tag}{half}", rpart(-d, tag, half), rpart(-d - 1, tag, half), zdev(1))
        if d < 3 or half == 1:
            push(f"r-{d + 1}{tag}{half}", rpart(d, tag, half), rpart(d + 1, tag, half), zdev(-1))

    def last(d, half):
        arrived(f"r+{d}p{half}", f"r-{d}p{half}")
        for n in range(2):
            at = pl.ds(6 * half + 3 * n, 3)
            way, below = ("-", 1) if half else ("+", -1)
            src = mid_p.at[pl.ds(((1 + below) + e) * PART + 6 * half + 3 * n, 3)]
            push(f"r{way}4p{n}", src, far_p.at[at], zdev(-below))

    def share(d, tag):
        push(f"e-{d}{tag}", rpart(-d, tag), rpart(-d, tag), edev)
        push(f"e+{d}{tag}", rpart(d, tag), rpart(d, tag), edev)

    def multiply(ref, d_of, devices, rows_of):
        groups = ref.shape[0] // (PART * len(devices))

        def one_group(j, carry):
            c = (z + d_of(j) + NZ) % NZ
            dx, dy = (c // 2 - x + NX) % NX, (c + y) % 2

            def one_row(i):
                slots = [(n, 2 * g + s) for n, g in enumerate(devices) for s in range(2)]
                ks = [lk[i, c * LSLOT + s] for _, s in slots]
                lhs = jnp.concatenate([lbuf[c, i, s] for _, s in slots], axis=1)
                for u in range(0, OSLOT, 2):
                    rhs = jnp.concatenate(
                        [
                            jnp.concatenate(
                                [
                                    ref[(j * len(devices) + n) * PART + code[i * OSLOT + u + v, k]]
                                    for v in range(2)
                                ],
                                axis=1,
                            )
                            for (n, _), k in zip(slots, ks)
                        ],
                        axis=0,
                    )
                    part = jnp.dot(lhs, rhs, preferred_element_type=jnp.float32)
                    acc[i, u] += part[:, :BLK]
                    acc[i, u + 1] += part[:, BLK:]

            def two_rows(i, carry):
                one_row(2 * i)
                one_row(2 * i + 1)
                return carry

            first, last = rows_of(dx, dy)
            lax.fori_loop(first // 2, last // 2, two_rows, 0)
            return carry

        if groups == 1:
            one_group(0, 0)
        else:
            lax.fori_loop(0, groups, one_group, 0)

    same, other, every = [h * 2, h * 2 + 1], [2 - h * 2, 3 - h * 2], range(4)
    products = {
        "near": (near, lambda j: j - 1, every),
        "next": (next_, lambda j: 4 * j - 2, every),
        "mid_o": (mid_o, lambda j: 6 * j - 3, same),
        "mid_p": (mid_p, lambda j: 6 * j - 3, other),
        "far_o": (far_o, lambda j: 4, same),
        "far_p": (far_p, lambda j: 4, [2 - h * 2 + e]),
        "far_q": (far_q, lambda j: 4, [3 - h * 2 - e]),
    }

    def rows_0(dx, dy):
        return jnp.where((dx != 2) & ((dy == 0) | (dx == 0)), 4, 0)

    def rows_2(dx, dy):
        return jnp.where(dy == 0, 4, jnp.where(dx == 2, 0, jnp.where(dx == 3, 2, 4)))

    def rows_3(dx, dy):
        return jnp.where((dx == 2) & (dy == 1), 0, 4)

    def nothing(dx, dy):
        return 0

    def everything(dx, dy):
        return 4

    def work(name, before, now):
        multiply(*products[name], lambda dx, dy: (before(dx, dy), now(dx, dy)))

    push("ma", rm.at[0], rm.at[1], edev)
    push("mh", rm.at[0], rm.at[2], hdev)
    push("na", lm.at[0], lm.at[1], ydev)
    for half in range(2):
        own = right.at[pl.ds(half * (RDEV // 2), RDEV // 2)]
        push(f"r+1o{half}", own, rpart(-1, "o", half), zdev(1))
        push(f"r-1o{half}", own, rpart(1, "o", half), zdev(-1))
    push("rh", right, rpart(0, "o"), hdev)
    push("l+1a", left.at[pl.ds(0, 2)], lpart(0, y, 0), xdev(1))
    push("l-1b", left.at[pl.ds(2, 2)], lpart(0, y, 1), xdev(-1))
    push("lya", left.at[pl.ds(0, 2)], lpart(0, y, 0), ydev)
    push("e0o", right, rpart(0, "o"), edev)
    arrived("mh")
    push("me", rm.at[2], rm.at[3], edev)
    arrived("na")
    ls[...] = lm[0] + lm[1]
    push("nb+1", ls, lc.at[0], xdev(1))
    push("nb-1", ls, lc.at[2], xdev(-1))
    push("l+1b", left.at[pl.ds(2, 2)], lpart(0, y, 1), xdev(1))
    push("l-1a", left.at[pl.ds(0, 2)], lpart(0, y, 0), xdev(-1))
    arrived("ma", "me")
    rc[0] = rm[0] + rm[1] + rm[2] + rm[3]
    push("mc+1", rc.at[0], rc.at[7], zdev(1))
    push("mc-1", rc.at[0], rc.at[1], zdev(-1))

    hop(1, "o", 0)
    acc[...] = jnp.zeros_like(acc)
    for ref in parts:
        for n in range(ref.shape[0] // PART):
            ref[n * PART + ZERO] = jnp.zeros((BLK, BLK), jnp.bfloat16)
    code_v[:, BLK:] = jnp.full((ROWS * OSLOT, BLK), ZERO, jnp.int32)
    arrived("mc+1", "mc-1")
    push("mc+2", rc.at[7], rc.at[6], zdev(1))
    push("mc-2", rc.at[1], rc.at[2], zdev(-1))
    hop(1, "o", 1)
    for d in (-1, 1):
        push(f"v{d}", rtail(d, "o"), rtail(d, "o"), hdev)
    push("lyb", left.at[pl.ds(2, 2)], lpart(0, y, 1), ydev)
    share(1, "o")
    arrived("rh")
    for half in range(2):
        push(f"r+1p{half}", rmost(0, half), rmost(-1, half), zdev(1))
        push(f"r-1p{half}", rmost(0, half), rmost(1, half), zdev(-1))
    push("e0p", rpart(0, "p"), rpart(0, "p"), edev)
    arrived("mc+2", "mc-2")
    push("mc+3", rc.at[6], rc.at[5], zdev(1))
    push("mc-3", rc.at[2], rc.at[3], zdev(-1))
    hop(2, "o", 0)
    arrived("l+1a", "l-1b", "nb+1", "nb-1")
    push("nb+2", lc.at[0], lc.at[1], xdev(1))
    push("l+2", lpart(-1, y, 0), lpart(-1, y, 0), xdev(1))
    push("l-2", lpart(1, y, 1), lpart(1, y, 1), xdev(-1))
    push("b-1", lpart(1, y, 1), lpart(1, y, 1), ydev)
    hop(2, "o", 1)
    share(2, "o")
    arrived("mc+3", "mc-3")
    push("mc+4", rc.at[5], rc.at[4], zdev(1))
    hop(1, "p", 0)
    arrived("lya")
    for i in range(2):
        push(f"a+1{i}", lrow(0, 1 - y, i), lrow(0, 1 - y, i), xdev(1))
        push(f"a-1{i}", lrow(0, 1 - y, i), lrow(0, 1 - y, i), xdev(-1))
    arrived("l+1b", "l-1a")
    push("b+1", lpart(-1, y, 1), lpart(-1, y, 1), ydev)
    arrived("v-1", "v1")
    hop(1, "p", 1)
    share(1, "p")
    hop(3, "o", 0)
    arrived("nb+2", "mc+4")
    right_table = rc[0]
    for d in range(1, NZ):
        right_table = right_table + rc[d]
    left_table = ls[...]
    for d in range(NX - 1):
        left_table = left_table + lc[d]
    lc[NX - 1] = jnp.where(left_table == 0, BLK, left_table - 1)
    wide_sub = lax.broadcasted_iota(jnp.int32, (ROWS * OSLOT, BLK), 0)
    wide_lane = lax.broadcasted_iota(jnp.int32, (ROWS * OSLOT, BLK), 1)
    wanted = jnp.full((ROWS * OSLOT, BLK), -1, jnp.int32)
    for i in range(ROWS):
        for u in range(OSLOT):
            value = jnp.where(u < pcnt[i], pidx[i, u] + 1, -1)
            wanted = jnp.where(wide_sub == i * OSLOT + u, value, wanted)
    found = jnp.full((ROWS * OSLOT, BLK), ZERO, jnp.int32)
    for t in range(RSLOT):
        found = jnp.where(right_table[t : t + 1, :] == wanted, (wide_lane % ROWS) * RSLOT + t, found)
    code_v[:, :BLK] = found
    to_code = pltpu.make_async_copy(code_v, code, local.at[8])
    to_code.start()
    to_lk = pltpu.make_async_copy(lc.at[NX - 1], lk, local.at[9])
    to_lk.start()

    hop(3, "o", 1)
    share(3, "o")
    own_left.wait()
    own_right.wait()
    to_code.wait()
    to_lk.wait()
    for tag in "op":
        arrived(f"e0{tag}", f"e-1{tag}", f"e+1{tag}")
    arrived("lyb")
    work("near", nothing, rows_0)
    hop(2, "p", 0)
    arrived("a+10", "a-10")
    push("a+20", lrow(-1, 1 - y, 0), lrow(-1, 1 - y, 0), xdev(1))
    hop(2, "p", 1)
    share(2, "p")
    arrived("b-1")
    push("b-2", lpart(1, 1 - y, 1), lpart(1, 1 - y, 1), xdev(-1))
    for tag in "op":
        arrived(f"e-2{tag}", f"e+2{tag}")
    work("next", nothing, rows_0)
    arrived("a+11", "a-11")
    push("a+21", lrow(-1, 1 - y, 1), lrow(-1, 1 - y, 1), xdev(1))
    arrived("r+4o0", "r-4o1")
    push("e4o", rpart(4, "o"), rpart(4, "o"), edev)
    arrived("l+2", "l-2", "e-3o", "e+3o")
    work("near", rows_0, rows_2)
    work("next", rows_0, rows_2)
    last(3, 0)
    work("mid_o", nothing, rows_2)
    last(3, 1)
    share(3, "p")
    arrived("b+1", "e4o")
    for name in ("near", "next", "mid_o", "far_o"):
        work(name, rows_2 if name != "far_o" else nothing, rows_3)
    arrived("a+20", "a+21", "b-2")
    for name in ("near", "next", "mid_o", "far_o"):
        work(name, rows_3, everything)
    arrived("e-3p", "e+3p")
    work("mid_p", nothing, everything)
    arrived("r+4p0", "r-4p0")
    push("e4p0", far_p.at[pl.ds(0, 3)], far_q.at[pl.ds(0, 3)], edev)
    push("e4p1", far_p.at[pl.ds(6, 3)], far_q.at[pl.ds(6, 3)], edev)
    arrived("r+4p1", "r-4p1")
    push("e4p2", far_p.at[pl.ds(3, 3)], far_q.at[pl.ds(3, 3)], edev)
    push("e4p3", far_p.at[pl.ds(9, 3)], far_q.at[pl.ds(9, 3)], edev)
    work("far_p", nothing, everything)
    arrived("e4p0", "e4p1", "e4p2", "e4p3")
    work("far_q", nothing, everything)

    for copy in copies.values():
        copy.wait_send()


def per_device(
    left_blocks,
    left_index,
    left_count,
    right_blocks,
    right_index,
    right_count,
    product_index,
    product_count,
):
    small = (
        left_index,
        left_count,
        right_index,
        right_count.reshape(ROWS),
        product_index,
        product_count.reshape(ROWS),
    )
    operands = (*small, left_blocks, right_blocks.reshape(RDEV, BLK, BLK))
    meta = functools.partial(pltpu.VMEM, dtype=jnp.int32)
    return pl.pallas_call(
        kernel,
        out_shape=pltpu.VMEM((ROWS, OSLOT, BLK, BLK), jnp.float32),
        in_specs=[pl.BlockSpec(memory_space=pl.ANY)] * 8,
        out_specs=pl.BlockSpec(memory_space=pltpu.VMEM),
        scratch_shapes=[
            pltpu.VMEM((8, ROWS, LSLOT, BLK, BLK), jnp.bfloat16),
        ]
        + [pltpu.VMEM((n * PART, BLK, BLK), jnp.bfloat16) for n in (12, 8, 4, 4, 2, 1, 1)]
        + [pltpu.SMEM(a.shape, jnp.int32) for a in small]
        + [
            meta((4, 8, BLK)),
            meta((NZ, 8, BLK)),
            meta((2, 8, BLK)),
            meta((8, BLK)),
            meta((NX, 8, BLK)),
            meta((ROWS * OSLOT, 2 * BLK)),
            pltpu.SMEM((ROWS * OSLOT, 2 * BLK), jnp.int32),
            pltpu.SMEM((8, BLK), jnp.int32),
            pltpu.SemaphoreType.DMA((COPIES,)),
            pltpu.SemaphoreType.DMA((COPIES,)),
            pltpu.SemaphoreType.DMA((10,)),
        ],
        compiler_params=pltpu.CompilerParams(
            collective_id=0, has_side_effects=True, vmem_limit_bytes=48 * 1024 * 1024
        ),
    )(*[pltpu.with_memory_space_constraint(a, pltpu.HBM) for a in operands])


def solution(mesh):
    return jax.shard_map(
        per_device,
        mesh=mesh,
        in_specs=(
            P("row", "col", None, None),
            P("row", "col"),
            P("row", "col"),
            P("row", "col", None, None),
            P("row", "col"),
            P("row", "col"),
            P("row", "col"),
            P("row", "col"),
        ),
        out_specs=P("row", "col", None, None),
        check_vma=False,
    )
```

```python
import functools

import jax
import jax.numpy as jnp
from jax import lax
from jax.experimental import pallas as pl
from jax.experimental.pallas import tpu as pltpu
from jax.sharding import PartitionSpec as P

MESH = pl.DeviceIdType.MESH
BLK = 128
NZ, NX = 8, 4
ROWS, LSLOT, RSLOT, OSLOT = 4, 8, 3, 6
RDEV = ROWS * RSLOT
ZERO = RDEV
PART = RDEV + 1
COPIES = 96
TAIL = 2


def kernel(*refs):
    small_in, (left, right, acc, lbuf), parts, rest = refs[:6], refs[6:10], refs[10:17], refs[17:]
    small, rest = rest[:6], rest[6:]
    near, next_, mid_o, mid_p, far_o, far_p, far_q = parts
    lidx, lcnt, ridx, rcnt, pidx, pcnt = small
    rm, rc, lm, ls, lc, code_v, code, lk, send, recv, local = rest
    row, col = lax.axis_index("row"), lax.axis_index("col")
    z, h, e = row // 4, (row // 2) % 2, row % 2
    x, y = col // 2, col % 2

    def zdev(d):
        return (((z + d) % NZ) * 4 + h * 2 + e, col)

    def xdev(d):
        return (row, ((x + d) % NX) * 2 + y)

    hdev = (z * 4 + (1 - h) * 2 + e, col)
    edev = (z * 4 + h * 2 + (1 - e), col)
    ydev = (row, x * 2 + (1 - y))

    barrier = pltpu.get_barrier_semaphore()
    partners = [zdev(1), zdev(-1), xdev(1), xdev(-1), hdev, edev, ydev]
    for dev in partners:
        pl.semaphore_signal(barrier, inc=1, device_id=dev, device_id_type=MESH)

    def rpart(d, tag, half=None):
        hh = h if tag == "o" else 1 - h
        if d in (-1, 0, 1):
            ref, at = near, (d + 1) * 4 + hh * 2 + e
        elif d in (-2, 2):
            ref, at = next_, (d + 2) + hh * 2 + e
        elif d in (-3, 3):
            ref, at = (mid_o if tag == "o" else mid_p), (d + 3) // 3 + e
        else:
            ref, at = (far_o, e) if tag == "o" else (far_p, 0)
        if half is None:
            return ref.at[pl.ds(at * PART, RDEV)]
        return ref.at[pl.ds(at * PART + half * (RDEV // 2), RDEV // 2)]

    def rtail(d, tag):
        hh = h if tag == "o" else 1 - h
        return near.at[pl.ds(((d + 1) * 4 + hh * 2 + e) * PART + RDEV - TAIL, TAIL)]

    def rmost(d, half):
        first = ((d + 1) * 4 + (1 - h) * 2 + e) * PART + half * (RDEV // 2)
        return near.at[pl.ds(first, RDEV // 2 - half * TAIL)]

    def lpart(dx, yy, half=None):
        at = ((x + dx) % NX) * 2 + yy
        if half is None:
            return lbuf.at[at]
        return lbuf.at[at, pl.ds(2 * half, 2)]

    def lrow(dx, yy, i):
        return lbuf.at[((x + dx) % NX) * 2 + yy, pl.ds(i, 1)]

    loads = [pltpu.make_async_copy(a, b, local.at[n]) for n, (a, b) in enumerate(zip(small_in, small))]
    for load in loads:
        load.start()
    own_left = pltpu.make_async_copy(left, lpart(0, y), local.at[6])
    own_left.start()
    own_right = pltpu.make_async_copy(right, rpart(0, "o"), local.at[7])
    own_right.start()
    for load in loads:
        load.wait()

    sub = lax.broadcasted_iota(jnp.int32, (8, BLK), 0)
    lane = lax.broadcasted_iota(jnp.int32, (8, BLK), 1)
    table = jnp.zeros((8, BLK), jnp.int32)
    for j in range(ROWS):
        for t in range(RSLOT):
            value = jnp.where(t < rcnt[j], ridx[j, t] + 1, 0)
            table = jnp.where((sub == t) & (lane == row * ROWS + j), value, table)
    rm[0] = table
    table = jnp.zeros((8, BLK), jnp.int32)
    for i in range(ROWS):
        for s in range(LSLOT):
            value = jnp.where(s % 2 < lcnt[i, s // 2], (col * 4 + s // 2) * ROWS + lidx[i, s] + 1, 0)
            table = jnp.where((sub == i) & (lane == col * LSLOT + s), value, table)
    lm[0] = table

    pl.semaphore_wait(barrier, len(partners))

    copies = {}

    def push(name, src, dst, dev):
        n = len(copies)
        copy = pltpu.make_async_remote_copy(
            src_ref=src,
            dst_ref=dst,
            send_sem=send.at[n],
            recv_sem=recv.at[n],
            device_id=dev,
            device_id_type=MESH,
        )
        copy.start()
        copies[name] = copy

    def arrived(*names):
        for name in names:
            copies[name].wait_recv()

    def hop(d, tag, half):
        arrived(f"r+{d}{tag}{half}", f"r-{d}{tag}{half}")
        if d < 3 or half == 0:
            push(f"r+{d + 1}{tag}{half}", rpart(-d, tag, half), rpart(-d - 1, tag, half), zdev(1))
        if d < 3 or half == 1:
            push(f"r-{d + 1}{tag}{half}", rpart(d, tag, half), rpart(d + 1, tag, half), zdev(-1))

    def last(d, half):
        arrived(f"r+{d}p{half}", f"r-{d}p{half}")
        for n in range(2):
            at = pl.ds(6 * half + 3 * n, 3)
            way, below = ("-", 1) if half else ("+", -1)
            src = mid_p.at[pl.ds(((1 + below) + e) * PART + 6 * half + 3 * n, 3)]
            push(f"r{way}4p{n}", src, far_p.at[at], zdev(-below))

    def share(d, tag):
        push(f"e-{d}{tag}", rpart(-d, tag), rpart(-d, tag), edev)
        push(f"e+{d}{tag}", rpart(d, tag), rpart(d, tag), edev)

    def multiply(ref, d_of, devices, rows_of):
        groups = ref.shape[0] // (PART * len(devices))

        def one_group(j, carry):
            c = (z + d_of(j) + NZ) % NZ
            dx, dy = (c // 2 - x + NX) % NX, (c + y) % 2

            def one_row(i):
                slots = [(n, 2 * g + s) for n, g in enumerate(devices) for s in range(2)]
                ks = [lk[i, c * LSLOT + s] for _, s in slots]
                lhs = jnp.concatenate([lbuf[c, i, s] for _, s in slots], axis=1)
                for u in range(0, OSLOT, 2):
                    rhs = jnp.concatenate(
                        [
                            jnp.concatenate(
                                [
                                    ref[(j * len(devices) + n) * PART + code[i * OSLOT + u + v, k]]
                                    for v in range(2)
                                ],
                                axis=1,
                            )
                            for (n, _), k in zip(slots, ks)
                        ],
                        axis=0,
                    )
                    part = jnp.dot(lhs, rhs, preferred_element_type=jnp.float32)
                    acc[i, u] += part[:, :BLK]
                    acc[i, u + 1] += part[:, BLK:]

            def two_rows(i, carry):
                one_row(2 * i)
                one_row(2 * i + 1)
                return carry

            first, last = rows_of(dx, dy)
            lax.fori_loop(first // 2, last // 2, two_rows, 0)
            return carry

        if groups == 1:
            one_group(0, 0)
        else:
            lax.fori_loop(0, groups, one_group, 0)

    same, other, every = [h * 2, h * 2 + 1], [2 - h * 2, 3 - h * 2], range(4)
    products = {
        "near": (near, lambda j: j - 1, every),
        "next": (next_, lambda j: 4 * j - 2, every),
        "mid_o": (mid_o, lambda j: 6 * j - 3, same),
        "mid_p": (mid_p, lambda j: 6 * j - 3, other),
        "far_o": (far_o, lambda j: 4, same),
        "far_p": (far_p, lambda j: 4, [2 - h * 2 + e]),
        "far_q": (far_q, lambda j: 4, [3 - h * 2 - e]),
    }

    def rows_0(dx, dy):
        return jnp.where((dx != 2) & ((dy == 0) | (dx == 0)), 4, 0)

    def rows_2(dx, dy):
        return jnp.where(dy == 0, 4, jnp.where(dx == 2, 0, jnp.where(dx == 3, 2, 4)))

    def rows_3(dx, dy):
        return jnp.where((dx == 2) & (dy == 1), 0, 4)

    def nothing(dx, dy):
        return 0

    def everything(dx, dy):
        return 4

    def work(name, before, now):
        multiply(*products[name], lambda dx, dy: (before(dx, dy), now(dx, dy)))

    push("ma", rm.at[0], rm.at[1], edev)
    push("mh", rm.at[0], rm.at[2], hdev)
    push("na", lm.at[0], lm.at[1], ydev)
    for half in range(2):
        own = right.at[pl.ds(half * (RDEV // 2), RDEV // 2)]
        push(f"r+1o{half}", own, rpart(-1, "o", half), zdev(1))
        push(f"r-1o{half}", own, rpart(1, "o", half), zdev(-1))
    push("rh", right, rpart(0, "o"), hdev)
    push("l+1a", left.at[pl.ds(0, 2)], lpart(0, y, 0), xdev(1))
    push("l-1b", left.at[pl.ds(2, 2)], lpart(0, y, 1), xdev(-1))
    push("lya", left.at[pl.ds(0, 2)], lpart(0, y, 0), ydev)
    push("e0o", right, rpart(0, "o"), edev)
    arrived("mh")
    push("me", rm.at[2], rm.at[3], edev)
    arrived("na")
    ls[...] = lm[0] + lm[1]
    push("nb+1", ls, lc.at[0], xdev(1))
    push("nb-1", ls, lc.at[2], xdev(-1))
    push("l+1b", left.at[pl.ds(2, 2)], lpart(0, y, 1), xdev(1))
    push("l-1a", left.at[pl.ds(0, 2)], lpart(0, y, 0), xdev(-1))
    arrived("ma", "me")
    rc[0] = rm[0] + rm[1] + rm[2] + rm[3]
    push("mc+1", rc.at[0], rc.at[7], zdev(1))
    push("mc-1", rc.at[0], rc.at[1], zdev(-1))

    hop(1, "o", 0)
    acc[...] = jnp.zeros_like(acc)
    for ref in parts:
        for n in range(ref.shape[0] // PART):
            ref[n * PART + ZERO] = jnp.zeros((BLK, BLK), jnp.bfloat16)
    code_v[:, BLK:] = jnp.full((ROWS * OSLOT, BLK), ZERO, jnp.int32)
    arrived("mc+1", "mc-1")
    push("mc+2", rc.at[7], rc.at[6], zdev(1))
    push("mc-2", rc.at[1], rc.at[2], zdev(-1))
    hop(1, "o", 1)
    for d in (-1, 1):
        push(f"v{d}", rtail(d, "o"), rtail(d, "o"), hdev)
    push("lyb", left.at[pl.ds(2, 2)], lpart(0, y, 1), ydev)
    share(1, "o")
    arrived("rh")
    for half in range(2):
        push(f"r+1p{half}", rmost(0, half), rmost(-1, half), zdev(1))
        push(f"r-1p{half}", rmost(0, half), rmost(1, half), zdev(-1))
    push("e0p", rpart(0, "p"), rpart(0, "p"), edev)
    arrived("mc+2", "mc-2")
    push("mc+3", rc.at[6], rc.at[5], zdev(1))
    push("mc-3", rc.at[2], rc.at[3], zdev(-1))
    hop(2, "o", 0)
    arrived("l+1a", "l-1b", "nb+1", "nb-1")
    push("nb+2", lc.at[0], lc.at[1], xdev(1))
    push("l+2", lpart(-1, y, 0), lpart(-1, y, 0), xdev(1))
    push("l-2", lpart(1, y, 1), lpart(1, y, 1), xdev(-1))
    push("b-1", lpart(1, y, 1), lpart(1, y, 1), ydev)
    hop(2, "o", 1)
    share(2, "o")
    arrived("mc+3", "mc-3")
    push("mc+4", rc.at[5], rc.at[4], zdev(1))
    hop(1, "p", 0)
    arrived("lya")
    for i in range(2):
        push(f"a+1{i}", lrow(0, 1 - y, i), lrow(0, 1 - y, i), xdev(1))
        push(f"a-1{i}", lrow(0, 1 - y, i), lrow(0, 1 - y, i), xdev(-1))
    arrived("l+1b", "l-1a")
    push("b+1", lpart(-1, y, 1), lpart(-1, y, 1), ydev)
    arrived("v-1", "v1")
    hop(1, "p", 1)
    share(1, "p")
    hop(3, "o", 0)
    arrived("nb+2", "mc+4")
    right_table = rc[0]
    for d in range(1, NZ):
        right_table = right_table + rc[d]
    left_table = ls[...]
    for d in range(NX - 1):
        left_table = left_table + lc[d]
    lc[NX - 1] = jnp.where(left_table == 0, BLK, left_table - 1)
    wide_sub = lax.broadcasted_iota(jnp.int32, (ROWS * OSLOT, BLK), 0)
    wide_lane = lax.broadcasted_iota(jnp.int32, (ROWS * OSLOT, BLK), 1)
    wanted = jnp.full((ROWS * OSLOT, BLK), -1, jnp.int32)
    for i in range(ROWS):
        for u in range(OSLOT):
            value = jnp.where(u < pcnt[i], pidx[i, u] + 1, -1)
            wanted = jnp.where(wide_sub == i * OSLOT + u, value, wanted)
    found = jnp.full((ROWS * OSLOT, BLK), ZERO, jnp.int32)
    for t in range(RSLOT):
        found = jnp.where(right_table[t : t + 1, :] == wanted, (wide_lane % ROWS) * RSLOT + t, found)
    code_v[:, :BLK] = found
    to_code = pltpu.make_async_copy(code_v, code, local.at[8])
    to_code.start()
    to_lk = pltpu.make_async_copy(lc.at[NX - 1], lk, local.at[9])
    to_lk.start()

    hop(3, "o", 1)
    share(3, "o")
    own_left.wait()
    own_right.wait()
    to_code.wait()
    to_lk.wait()
    for tag in "op":
        arrived(f"e0{tag}", f"e-1{tag}", f"e+1{tag}")
    arrived("lyb")
    work("near", nothing, rows_0)
    hop(2, "p", 0)
    arrived("a+10", "a-10")
    push("a+20", lrow(-1, 1 - y, 0), lrow(-1, 1 - y, 0), xdev(1))
    hop(2, "p", 1)
    share(2, "p")
    arrived("b-1")
    push("b-2", lpart(1, 1 - y, 1), lpart(1, 1 - y, 1), xdev(-1))
    for tag in "op":
        arrived(f"e-2{tag}", f"e+2{tag}")
    work("next", nothing, rows_0)
    arrived("a+11", "a-11")
    push("a+21", lrow(-1, 1 - y, 1), lrow(-1, 1 - y, 1), xdev(1))
    arrived("r+4o0", "r-4o1")
    push("e4o", rpart(4, "o"), rpart(4, "o"), edev)
    arrived("l+2", "l-2", "e-3o", "e+3o")
    work("near", rows_0, rows_2)
    work("next", rows_0, rows_2)
    last(3, 0)
    work("mid_o", nothing, rows_2)
    last(3, 1)
    share(3, "p")
    arrived("b+1", "e4o")
    for name in ("near", "next", "mid_o", "far_o"):
        work(name, rows_2 if name != "far_o" else nothing, rows_3)
    arrived("e-3p", "e+3p")
    work("mid_p", nothing, rows_3)
    arrived("r+4p0", "r-4p0")
    push("e4p0", far_p.at[pl.ds(0, 3)], far_q.at[pl.ds(0, 3)], edev)
    push("e4p1", far_p.at[pl.ds(6, 3)], far_q.at[pl.ds(6, 3)], edev)
    arrived("r+4p1", "r-4p1")
    push("e4p2", far_p.at[pl.ds(3, 3)], far_q.at[pl.ds(3, 3)], edev)
    push("e4p3", far_p.at[pl.ds(9, 3)], far_q.at[pl.ds(9, 3)], edev)
    work("far_p", nothing, rows_3)
    arrived("a+20", "a+21", "b-2")
    for name in ("near", "next", "mid_o", "mid_p", "far_o", "far_p"):
        work(name, rows_3, everything)
    arrived("e4p0", "e4p1", "e4p2", "e4p3")
    work("far_q", nothing, everything)

    for copy in copies.values():
        copy.wait_send()


def per_device(
    left_blocks,
    left_index,
    left_count,
    right_blocks,
    right_index,
    right_count,
    product_index,
    product_count,
):
    small = (
        left_index,
        left_count,
        right_index,
        right_count.reshape(ROWS),
        product_index,
        product_count.reshape(ROWS),
    )
    operands = (*small, left_blocks, right_blocks.reshape(RDEV, BLK, BLK))
    meta = functools.partial(pltpu.VMEM, dtype=jnp.int32)
    return pl.pallas_call(
        kernel,
        out_shape=pltpu.VMEM((ROWS, OSLOT, BLK, BLK), jnp.float32),
        in_specs=[pl.BlockSpec(memory_space=pl.ANY)] * 8,
        out_specs=pl.BlockSpec(memory_space=pltpu.VMEM),
        scratch_shapes=[
            pltpu.VMEM((8, ROWS, LSLOT, BLK, BLK), jnp.bfloat16),
        ]
        + [pltpu.VMEM((n * PART, BLK, BLK), jnp.bfloat16) for n in (12, 8, 4, 4, 2, 1, 1)]
        + [pltpu.SMEM(a.shape, jnp.int32) for a in small]
        + [
            meta((4, 8, BLK)),
            meta((NZ, 8, BLK)),
            meta((2, 8, BLK)),
            meta((8, BLK)),
            meta((NX, 8, BLK)),
            meta((ROWS * OSLOT, 2 * BLK)),
            pltpu.SMEM((ROWS * OSLOT, 2 * BLK), jnp.int32),
            pltpu.SMEM((8, BLK), jnp.int32),
            pltpu.SemaphoreType.DMA((COPIES,)),
            pltpu.SemaphoreType.DMA((COPIES,)),
            pltpu.SemaphoreType.DMA((10,)),
        ],
        compiler_params=pltpu.CompilerParams(
            collective_id=0, has_side_effects=True, vmem_limit_bytes=48 * 1024 * 1024
        ),
    )(*[pltpu.with_memory_space_constraint(a, pltpu.HBM) for a in operands])


def solution(mesh):
    return jax.shard_map(
        per_device,
        mesh=mesh,
        in_specs=(
            P("row", "col", None, None),
            P("row", "col"),
            P("row", "col"),
            P("row", "col", None, None),
            P("row", "col"),
            P("row", "col"),
            P("row", "col"),
            P("row", "col"),
        ),
        out_specs=P("row", "col", None, None),
        check_vma=False,
    )
```

```python
import functools

import jax
import jax.numpy as jnp
from jax import lax
from jax.experimental import pallas as pl
from jax.experimental.pallas import tpu as pltpu
from jax.sharding import PartitionSpec as P

MESH = pl.DeviceIdType.MESH
BLK = 128
NZ, NX = 8, 4
ROWS, LSLOT, RSLOT, OSLOT = 4, 8, 3, 6
RDEV = ROWS * RSLOT
ZERO = RDEV
PART = RDEV + 1
COPIES = 96
TAIL = 2


def kernel(*refs):
    small_in, (left, right, acc, lbuf), parts, rest = refs[:6], refs[6:10], refs[10:17], refs[17:]
    small, rest = rest[:6], rest[6:]
    near, next_, mid_o, mid_p, far_o, far_p, far_q = parts
    lidx, lcnt, ridx, rcnt, pidx, pcnt = small
    rm, rc, lm, ls, lc, code_v, code, lk, send, recv, local = rest
    row, col = lax.axis_index("row"), lax.axis_index("col")
    z, h, e = row // 4, (row // 2) % 2, row % 2
    x, y = col // 2, col % 2

    def zdev(d):
        return (((z + d) % NZ) * 4 + h * 2 + e, col)

    def xdev(d):
        return (row, ((x + d) % NX) * 2 + y)

    hdev = (z * 4 + (1 - h) * 2 + e, col)
    edev = (z * 4 + h * 2 + (1 - e), col)
    ydev = (row, x * 2 + (1 - y))

    barrier = pltpu.get_barrier_semaphore()
    partners = [zdev(1), zdev(-1), xdev(1), xdev(-1), hdev, edev, ydev]
    for dev in partners:
        pl.semaphore_signal(barrier, inc=1, device_id=dev, device_id_type=MESH)

    def rpart(d, tag, half=None):
        hh = h if tag == "o" else 1 - h
        if d in (-1, 0, 1):
            ref, at = near, (d + 1) * 4 + hh * 2 + e
        elif d in (-2, 2):
            ref, at = next_, (d + 2) + hh * 2 + e
        elif d in (-3, 3):
            ref, at = (mid_o if tag == "o" else mid_p), (d + 3) // 3 + e
        else:
            ref, at = (far_o, e) if tag == "o" else (far_p, 0)
        if half is None:
            return ref.at[pl.ds(at * PART, RDEV)]
        return ref.at[pl.ds(at * PART + half * (RDEV // 2), RDEV // 2)]

    def rtail(d, tag):
        hh = h if tag == "o" else 1 - h
        return near.at[pl.ds(((d + 1) * 4 + hh * 2 + e) * PART + RDEV - TAIL, TAIL)]

    def rmost(d, half):
        first = ((d + 1) * 4 + (1 - h) * 2 + e) * PART + half * (RDEV // 2)
        return near.at[pl.ds(first, RDEV // 2 - half * TAIL)]

    def lpart(dx, yy, half=None):
        at = ((x + dx) % NX) * 2 + yy
        if half is None:
            return lbuf.at[at]
        return lbuf.at[at, pl.ds(2 * half, 2)]

    def lrow(dx, yy, i):
        return lbuf.at[((x + dx) % NX) * 2 + yy, pl.ds(i, 1)]

    loads = [pltpu.make_async_copy(a, b, local.at[n]) for n, (a, b) in enumerate(zip(small_in, small))]
    for load in loads:
        load.start()
    own_left = pltpu.make_async_copy(left, lpart(0, y), local.at[6])
    own_left.start()
    own_right = pltpu.make_async_copy(right, rpart(0, "o"), local.at[7])
    own_right.start()
    pl.semaphore_wait(barrier, len(partners))

    copies = {}

    def push(name, src, dst, dev):
        n = len(copies)
        copy = pltpu.make_async_remote_copy(
            src_ref=src,
            dst_ref=dst,
            send_sem=send.at[n],
            recv_sem=recv.at[n],
            device_id=dev,
            device_id_type=MESH,
        )
        copy.start()
        copies[name] = copy

    def arrived(*names):
        for name in names:
            copies[name].wait_recv()

    def hop(d, tag, half):
        arrived(f"r+{d}{tag}{half}", f"r-{d}{tag}{half}")
        if d < 3 or half == 0:
            push(f"r+{d + 1}{tag}{half}", rpart(-d, tag, half), rpart(-d - 1, tag, half), zdev(1))
        if d < 3 or half == 1:
            push(f"r-{d + 1}{tag}{half}", rpart(d, tag, half), rpart(d + 1, tag, half), zdev(-1))

    def last(d, half):
        arrived(f"r+{d}p{half}", f"r-{d}p{half}")
        for n in range(2):
            at = pl.ds(6 * half + 3 * n, 3)
            way, below = ("-", 1) if half else ("+", -1)
            src = mid_p.at[pl.ds(((1 + below) + e) * PART + 6 * half + 3 * n, 3)]
            push(f"r{way}4p{n}", src, far_p.at[at], zdev(-below))

    def share(d, tag):
        push(f"e-{d}{tag}", rpart(-d, tag), rpart(-d, tag), edev)
        push(f"e+{d}{tag}", rpart(d, tag), rpart(d, tag), edev)

    def multiply(ref, d_of, devices, rows_of):
        groups = ref.shape[0] // (PART * len(devices))

        def one_group(j, carry):
            c = (z + d_of(j) + NZ) % NZ
            dx, dy = (c // 2 - x + NX) % NX, (c + y) % 2

            def one_row(i):
                slots = [(n, 2 * g + s) for n, g in enumerate(devices) for s in range(2)]
                ks = [lk[i, c * LSLOT + s] for _, s in slots]
                lhs = jnp.concatenate([lbuf[c, i, s] for _, s in slots], axis=1)
                for u in range(0, OSLOT, 2):
                    rhs = jnp.concatenate(
                        [
                            jnp.concatenate(
                                [
                                    ref[(j * len(devices) + n) * PART + code[i * OSLOT + u + v, k]]
                                    for v in range(2)
                                ],
                                axis=1,
                            )
                            for (n, _), k in zip(slots, ks)
                        ],
                        axis=0,
                    )
                    part = jnp.dot(lhs, rhs, preferred_element_type=jnp.float32)
                    acc[i, u] += part[:, :BLK]
                    acc[i, u + 1] += part[:, BLK:]

            def two_rows(i, carry):
                one_row(2 * i)
                one_row(2 * i + 1)
                return carry

            first, last = rows_of(dx, dy)
            lax.fori_loop(first // 2, last // 2, two_rows, 0)
            return carry

        if groups == 1:
            one_group(0, 0)
        else:
            lax.fori_loop(0, groups, one_group, 0)

    same, other, every = [h * 2, h * 2 + 1], [2 - h * 2, 3 - h * 2], range(4)
    products = {
        "near": (near, lambda j: j - 1, every),
        "next": (next_, lambda j: 4 * j - 2, every),
        "mid_o": (mid_o, lambda j: 6 * j - 3, same),
        "mid_p": (mid_p, lambda j: 6 * j - 3, other),
        "far_o": (far_o, lambda j: 4, same),
        "far_p": (far_p, lambda j: 4, [2 - h * 2 + e]),
        "far_q": (far_q, lambda j: 4, [3 - h * 2 - e]),
    }

    def rows_0(dx, dy):
        return jnp.where((dx != 2) & ((dy == 0) | (dx == 0)), 4, 0)

    def rows_2(dx, dy):
        return jnp.where(dy == 0, 4, jnp.where(dx == 2, 0, jnp.where(dx == 3, 2, 4)))

    def rows_3(dx, dy):
        return jnp.where((dx == 2) & (dy == 1), 0, 4)

    def nothing(dx, dy):
        return 0

    def everything(dx, dy):
        return 4

    def work(name, before, now):
        multiply(*products[name], lambda dx, dy: (before(dx, dy), now(dx, dy)))

    for half in range(2):
        own = right.at[pl.ds(half * (RDEV // 2), RDEV // 2)]
        push(f"r+1o{half}", own, rpart(-1, "o", half), zdev(1))
        push(f"r-1o{half}", own, rpart(1, "o", half), zdev(-1))
    push("l+1a", left.at[pl.ds(0, 2)], lpart(0, y, 0), xdev(1))
    push("l-1b", left.at[pl.ds(2, 2)], lpart(0, y, 1), xdev(-1))

    for load in loads:
        load.wait()

    sub = lax.broadcasted_iota(jnp.int32, (8, BLK), 0)
    lane = lax.broadcasted_iota(jnp.int32, (8, BLK), 1)
    table = jnp.zeros((8, BLK), jnp.int32)
    for j in range(ROWS):
        for t in range(RSLOT):
            value = jnp.where(t < rcnt[j], ridx[j, t] + 1, 0)
            table = jnp.where((sub == t) & (lane == row * ROWS + j), value, table)
    rm[0] = table
    table = jnp.zeros((8, BLK), jnp.int32)
    for i in range(ROWS):
        for s in range(LSLOT):
            value = jnp.where(s % 2 < lcnt[i, s // 2], (col * 4 + s // 2) * ROWS + lidx[i, s] + 1, 0)
            table = jnp.where((sub == i) & (lane == col * LSLOT + s), value, table)
    lm[0] = table

    push("ma", rm.at[0], rm.at[1], edev)
    push("mh", rm.at[0], rm.at[2], hdev)
    push("na", lm.at[0], lm.at[1], ydev)
    push("rh", right, rpart(0, "o"), hdev)
    push("lya", left.at[pl.ds(0, 2)], lpart(0, y, 0), ydev)
    push("e0o", right, rpart(0, "o"), edev)
    arrived("mh")
    push("me", rm.at[2], rm.at[3], edev)
    arrived("na")
    ls[...] = lm[0] + lm[1]
    push("nb+1", ls, lc.at[0], xdev(1))
    push("nb-1", ls, lc.at[2], xdev(-1))
    push("l+1b", left.at[pl.ds(2, 2)], lpart(0, y, 1), xdev(1))
    push("l-1a", left.at[pl.ds(0, 2)], lpart(0, y, 0), xdev(-1))
    arrived("ma", "me")
    rc[0] = rm[0] + rm[1] + rm[2] + rm[3]
    push("mc+1", rc.at[0], rc.at[7], zdev(1))
    push("mc-1", rc.at[0], rc.at[1], zdev(-1))

    hop(1, "o", 0)
    acc[...] = jnp.zeros_like(acc)
    for ref in parts:
        for n in range(ref.shape[0] // PART):
            ref[n * PART + ZERO] = jnp.zeros((BLK, BLK), jnp.bfloat16)
    code_v[:, BLK:] = jnp.full((ROWS * OSLOT, BLK), ZERO, jnp.int32)
    arrived("mc+1", "mc-1")
    push("mc+2", rc.at[7], rc.at[6], zdev(1))
    push("mc-2", rc.at[1], rc.at[2], zdev(-1))
    hop(1, "o", 1)
    for d in (-1, 1):
        push(f"v{d}", rtail(d, "o"), rtail(d, "o"), hdev)
    push("lyb", left.at[pl.ds(2, 2)], lpart(0, y, 1), ydev)
    share(1, "o")
    arrived("rh")
    for half in range(2):
        push(f"r+1p{half}", rmost(0, half), rmost(-1, half), zdev(1))
        push(f"r-1p{half}", rmost(0, half), rmost(1, half), zdev(-1))
    push("e0p", rpart(0, "p"), rpart(0, "p"), edev)
    arrived("mc+2", "mc-2")
    push("mc+3", rc.at[6], rc.at[5], zdev(1))
    push("mc-3", rc.at[2], rc.at[3], zdev(-1))
    hop(2, "o", 0)
    arrived("l+1a", "l-1b", "nb+1", "nb-1")
    push("nb+2", lc.at[0], lc.at[1], xdev(1))
    push("l+2", lpart(-1, y, 0), lpart(-1, y, 0), xdev(1))
    push("l-2", lpart(1, y, 1), lpart(1, y, 1), xdev(-1))
    push("b-1", lpart(1, y, 1), lpart(1, y, 1), ydev)
    hop(2, "o", 1)
    share(2, "o")
    arrived("mc+3", "mc-3")
    push("mc+4", rc.at[5], rc.at[4], zdev(1))
    hop(1, "p", 0)
    arrived("lya")
    for i in range(2):
        push(f"a+1{i}", lrow(0, 1 - y, i), lrow(0, 1 - y, i), xdev(1))
        push(f"a-1{i}", lrow(0, 1 - y, i), lrow(0, 1 - y, i), xdev(-1))
    arrived("l+1b", "l-1a")
    push("b+1", lpart(-1, y, 1), lpart(-1, y, 1), ydev)
    arrived("v-1", "v1")
    hop(1, "p", 1)
    share(1, "p")
    hop(3, "o", 0)
    arrived("nb+2", "mc+4")
    right_table = rc[0]
    for d in range(1, NZ):
        right_table = right_table + rc[d]
    left_table = ls[...]
    for d in range(NX - 1):
        left_table = left_table + lc[d]
    lc[NX - 1] = jnp.where(left_table == 0, BLK, left_table - 1)
    wide_sub = lax.broadcasted_iota(jnp.int32, (ROWS * OSLOT, BLK), 0)
    wide_lane = lax.broadcasted_iota(jnp.int32, (ROWS * OSLOT, BLK), 1)
    wanted = jnp.full((ROWS * OSLOT, BLK), -1, jnp.int32)
    for i in range(ROWS):
        for u in range(OSLOT):
            value = jnp.where(u < pcnt[i], pidx[i, u] + 1, -1)
            wanted = jnp.where(wide_sub == i * OSLOT + u, value, wanted)
    found = jnp.full((ROWS * OSLOT, BLK), ZERO, jnp.int32)
    for t in range(RSLOT):
        found = jnp.where(right_table[t : t + 1, :] == wanted, (wide_lane % ROWS) * RSLOT + t, found)
    code_v[:, :BLK] = found
    to_code = pltpu.make_async_copy(code_v, code, local.at[8])
    to_code.start()
    to_lk = pltpu.make_async_copy(lc.at[NX - 1], lk, local.at[9])
    to_lk.start()

    hop(3, "o", 1)
    share(3, "o")
    own_left.wait()
    own_right.wait()
    to_code.wait()
    to_lk.wait()
    for tag in "op":
        arrived(f"e0{tag}", f"e-1{tag}", f"e+1{tag}")
    arrived("lyb")
    work("near", nothing, rows_0)
    hop(2, "p", 0)
    arrived("a+10", "a-10")
    push("a+20", lrow(-1, 1 - y, 0), lrow(-1, 1 - y, 0), xdev(1))
    hop(2, "p", 1)
    share(2, "p")
    arrived("b-1")
    push("b-2", lpart(1, 1 - y, 1), lpart(1, 1 - y, 1), xdev(-1))
    for tag in "op":
        arrived(f"e-2{tag}", f"e+2{tag}")
    work("next", nothing, rows_0)
    arrived("a+11", "a-11")
    push("a+21", lrow(-1, 1 - y, 1), lrow(-1, 1 - y, 1), xdev(1))
    arrived("r+4o0", "r-4o1")
    push("e4o", rpart(4, "o"), rpart(4, "o"), edev)
    arrived("l+2", "l-2", "e-3o", "e+3o")
    work("near", rows_0, rows_2)
    work("next", rows_0, rows_2)
    last(3, 0)
    work("mid_o", nothing, rows_2)
    last(3, 1)
    share(3, "p")
    arrived("b+1", "e4o")
    for name in ("near", "next", "mid_o", "far_o"):
        work(name, rows_2 if name != "far_o" else nothing, rows_3)
    arrived("e-3p", "e+3p")
    work("mid_p", nothing, rows_3)
    arrived("r+4p0", "r-4p0")
    push("e4p0", far_p.at[pl.ds(0, 3)], far_q.at[pl.ds(0, 3)], edev)
    push("e4p1", far_p.at[pl.ds(6, 3)], far_q.at[pl.ds(6, 3)], edev)
    arrived("r+4p1", "r-4p1")
    push("e4p2", far_p.at[pl.ds(3, 3)], far_q.at[pl.ds(3, 3)], edev)
    push("e4p3", far_p.at[pl.ds(9, 3)], far_q.at[pl.ds(9, 3)], edev)
    work("far_p", nothing, rows_3)
    arrived("a+20", "a+21", "b-2")
    for name in ("near", "next", "mid_o", "mid_p", "far_o", "far_p"):
        work(name, rows_3, everything)
    arrived("e4p0", "e4p1", "e4p2", "e4p3")
    work("far_q", nothing, everything)

    for copy in copies.values():
        copy.wait_send()


def per_device(
    left_blocks,
    left_index,
    left_count,
    right_blocks,
    right_index,
    right_count,
    product_index,
    product_count,
):
    small = (
        left_index,
        left_count,
        right_index,
        right_count.reshape(ROWS),
        product_index,
        product_count.reshape(ROWS),
    )
    operands = (*small, left_blocks, right_blocks.reshape(RDEV, BLK, BLK))
    meta = functools.partial(pltpu.VMEM, dtype=jnp.int32)
    return pl.pallas_call(
        kernel,
        out_shape=pltpu.VMEM((ROWS, OSLOT, BLK, BLK), jnp.float32),
        in_specs=[pl.BlockSpec(memory_space=pl.ANY)] * 8,
        out_specs=pl.BlockSpec(memory_space=pltpu.VMEM),
        scratch_shapes=[
            pltpu.VMEM((8, ROWS, LSLOT, BLK, BLK), jnp.bfloat16),
        ]
        + [pltpu.VMEM((n * PART, BLK, BLK), jnp.bfloat16) for n in (12, 8, 4, 4, 2, 1, 1)]
        + [pltpu.SMEM(a.shape, jnp.int32) for a in small]
        + [
            meta((4, 8, BLK)),
            meta((NZ, 8, BLK)),
            meta((2, 8, BLK)),
            meta((8, BLK)),
            meta((NX, 8, BLK)),
            meta((ROWS * OSLOT, 2 * BLK)),
            pltpu.SMEM((ROWS * OSLOT, 2 * BLK), jnp.int32),
            pltpu.SMEM((8, BLK), jnp.int32),
            pltpu.SemaphoreType.DMA((COPIES,)),
            pltpu.SemaphoreType.DMA((COPIES,)),
            pltpu.SemaphoreType.DMA((10,)),
        ],
        compiler_params=pltpu.CompilerParams(
            collective_id=0, has_side_effects=True, vmem_limit_bytes=48 * 1024 * 1024
        ),
    )(*[pltpu.with_memory_space_constraint(a, pltpu.HBM) for a in operands])


def solution(mesh):
    return jax.shard_map(
        per_device,
        mesh=mesh,
        in_specs=(
            P("row", "col", None, None),
            P("row", "col"),
            P("row", "col"),
            P("row", "col", None, None),
            P("row", "col"),
            P("row", "col"),
            P("row", "col"),
            P("row", "col"),
        ),
        out_specs=P("row", "col", None, None),
        check_vma=False,
    )
```
